32 devices in a mesh: seq: 4 (over y, x), head: 8 (over z, core).
Axes of the slice: x: 2, y: 2, z: 4, core: 2. Of those that a mesh axis runs over, the one named last changes fastest.
Arguments:
- out_grad: bfloat16 [2048, 8192], P('seq'), may hold values from -6 to 6
- out_weight: bfloat16 [8192, 8192], P(None, 'head'), may hold values from -0.0625 to 0.0625
- gate_input: bfloat16 [2048, 8192], P('seq', 'head'), may hold values from -6 to 6
- scan_output: bfloat16 [2048, 8192], P('seq', 'head'), may hold values from -6 to 6
- step_size: float32 [2048, 128], P('seq', 'head'), may hold values from 0.5 to 2
- log_decay: float32 [2048, 128], P('seq', 'head'), may hold values from -1 to 0
- input_map: bfloat16 [2048, 4, 256], P('seq'), may hold values from -0.375 to 0.375
- output_map: bfloat16 [2048, 4, 256], P('seq'), may hold values from -0.375 to 0.375
- skip_gain: float32 [128], P('head'), may hold values from 0.5 to 1.5
Outputs:
- input_grad: bfloat16 [2048, 8192], P('seq', 'head')
- gate_grad: bfloat16 [2048, 8192], P('seq', 'head')
- weight_grad: bfloat16 [8192, 8192], P(None, 'head')
The draws below stay inside these ranges and needn't reach their ends.
All inputs are finite; a program needn't handle non-finite values.
Results may differ from the reference program's by a relative error of at most 0.02.
Values may be sent and summed in bfloat16 or wider, within the bound.
A program may use at most 192 MiB of HBM per device.

```python
import math
from functools import partial
import jax
import jax.numpy as jnp
from jax import lax

D = 8192
HEAD_COUNT = 128
P_SIZE = 64
N = 256
G = 4
L_DEV = 512
TOKEN_COUNT = 2048
N_SEQ = 4


def draw_log_decay(key, part):
    random_subkeys = jax.random.split(key, 6)
    fast_share = 0.5
    fast_head = jax.random.uniform(random_subkeys[0], (HEAD_COUNT,)) < fast_share
    fast_rate = jax.random.uniform(random_subkeys[1], (HEAD_COUNT,), minval=0.06, maxval=0.1)
    slow_rate = jnp.exp(jax.random.uniform(random_subkeys[2], (HEAD_COUNT,), minval=math.log(0.1), maxval=math.log(0.8))) / TOKEN_COUNT
    decay_speed = jnp.where(fast_head, fast_rate, slow_rate)
    jaggedness = jax.random.uniform(random_subkeys[3], (TOKEN_COUNT, HEAD_COUNT), minval=0.5, maxval=1.5)
    spike_positions = jax.random.randint(random_subkeys[4], (3,), 0, TOKEN_COUNT)
    spike_selected = jnp.any(jnp.arange(TOKEN_COUNT)[:, None] == spike_positions[None, :], axis=1)
    spike_magnitude = jax.random.uniform(random_subkeys[5], (TOKEN_COUNT, HEAD_COUNT), minval=0.22, maxval=0.5)
    logarithm_values = -decay_speed[None, :] * jaggedness - jnp.where(spike_selected[:, None], spike_magnitude, 0.0)
    return logarithm_values.astype(jnp.float32)


def block_levels(own_key, extent, cuts, smallest, largest):
    def one(axis_at, parts):
        heights = jax.random.uniform(jax.random.fold_in(jax.random.fold_in(own_key, 6), axis_at), (parts,), jnp.float32, smallest / len(cuts), largest / len(cuts))
        return jnp.repeat(jnp.exp(heights), extent[axis_at] // parts).reshape((-1,) + (1,) * (len(extent) - axis_at - 1))

    factor_of = one(*cuts[0])
    for cut in cuts[1:]:
        factor_of = factor_of * one(*cut)
    return factor_of


def centred(stream_key, dims, deviation, bound, cuts=(), held_as=jnp.bfloat16):
    values = deviation * jax.random.normal(stream_key, dims, jnp.float32)
    if cuts:
        values = values * block_levels(stream_key, dims, cuts, -0.22, 0.18)
    return jnp.clip(values, -bound, bound).astype(held_as)


def setup_inputs(seed: int = 0) -> dict:
    splits = jax.random.split(jax.random.key(seed), 10)
    out_grad = centred(splits[0], (TOKEN_COUNT, D), 1.0, 6.0, ((0, 4),))
    out_weight = centred(splits[1], (HEAD_COUNT * P_SIZE, D), (HEAD_COUNT * P_SIZE) ** -0.5, 0.0625, ((1, 8),))
    gate_input = centred(splits[2], (TOKEN_COUNT, HEAD_COUNT * P_SIZE), 1.0, 6.0, ((0, 4), (1, 8)))
    scan_output = centred(splits[3], (TOKEN_COUNT, HEAD_COUNT * P_SIZE), 1.0, 6.0, ((0, 4), (1, 8)))
    step_size = jnp.clip(0.5 + 1.5 * jax.random.uniform(splits[4], (TOKEN_COUNT, HEAD_COUNT), jnp.float32) ** block_levels(splits[4], (TOKEN_COUNT, HEAD_COUNT), ((0, 4), (1, 8)), -0.2, 0.2), 0.5, 2.0)
    log_decay = draw_log_decay(jax.random.fold_in(splits[9], 71), 0)
    input_map = centred(splits[6], (TOKEN_COUNT, G, N), N ** -0.5, 0.375, ((0, 4),))
    output_map = centred(splits[7], (TOKEN_COUNT, G, N), N ** -0.5, 0.375, ((0, 4),))
    skip_gain = jnp.clip(0.5 + 1.0 * jax.random.uniform(splits[8], (HEAD_COUNT,), jnp.float32) ** block_levels(splits[8], (HEAD_COUNT,), ((0, 8),), -0.2, 0.2), 0.5, 1.5)
    return {"out_grad": out_grad, "out_weight": out_weight, "gate_input": gate_input, "scan_output": scan_output, "step_size": step_size, "log_decay": log_decay, "input_map": input_map, "output_map": output_map, "skip_gain": skip_gain}


highest = lax.Precision.HIGHEST

def block_grads(skip_gain, carried, inputs):
    decay_block, grad_block, step_block, in_block, out_block = inputs
    heads_group = HEAD_COUNT // G
    cumulative = jnp.cumsum(decay_block, axis=0)
    block_total = cumulative[-1]
    intersection = jnp.einsum('tgn,sgn->gts', in_block.astype(jnp.float32), out_block.astype(jnp.float32), precision=highest)
    intersection = jnp.repeat(intersection, heads_group, axis=0)
    positions = jnp.arange(decay_block.shape[0])
    upper_mask = positions[:, None] <= positions[None, :]
    spread = cumulative.T[:, None, :] - cumulative.T[:, :, None]
    factor = jnp.where(upper_mask[None], jnp.exp(jnp.minimum(spread, 0.0)), 0.0)
    weights = (intersection * factor).astype(jnp.bfloat16)
    grad_float = grad_block.astype(jnp.float32)
    inside_term = jnp.einsum('hts,shp->thp', weights.astype(jnp.float32), grad_float, precision=highest)
    in_heads = jnp.repeat(in_block.astype(jnp.float32), heads_group, axis=1)
    out_heads = jnp.repeat(out_block.astype(jnp.float32), heads_group, axis=1)
    carried_term = jnp.einsum('hpn,thn->thp', carried, in_heads, precision=highest)
    tail_decay = jnp.exp(block_total[None, :] - cumulative)
    result = step_block[:, :, None] * (inside_term + tail_decay[:, :, None] * carried_term) + skip_gain[None, :, None] * grad_float
    weighted = grad_float * jnp.exp(cumulative)[:, :, None]
    local_term = jnp.einsum('thp,thn->hpn', weighted, out_heads, precision=highest)
    passed = local_term + jnp.exp(block_total)[:, None, None] * carried
    return (passed, result.astype(jnp.bfloat16))

def reference(out_grad, out_weight, gate_input, scan_output, step_size, log_decay, input_map, output_map, skip_gain):
    upstream = jnp.dot(out_grad, out_weight.T, preferred_element_type=jnp.float32)
    gate_value = gate_input.astype(jnp.float32)
    sigmoid_gate = jax.nn.sigmoid(gate_value)
    silu_gate = gate_value * sigmoid_gate
    saved_output = scan_output.astype(jnp.float32)
    gated_rows = (saved_output * silu_gate).astype(jnp.bfloat16)
    gate_grad = (upstream * saved_output * sigmoid_gate * (1.0 + gate_value * (1.0 - sigmoid_gate))).astype(jnp.bfloat16)
    scan_grad = (upstream * silu_gate).astype(jnp.bfloat16)
    grad_scale = 1.0 / math.sqrt(TOKEN_COUNT)

    def add_block(block_index, total):
        start = (block_index * L_DEV).astype(jnp.int32)
        rows_gated = lax.dynamic_slice_in_dim(gated_rows, start, L_DEV, 0)
        rows_grad = lax.dynamic_slice_in_dim(out_grad, start, L_DEV, 0)
        block_part = (jnp.dot(rows_gated.T, rows_grad, preferred_element_type=jnp.float32) * grad_scale).astype(jnp.bfloat16)
        return total + block_part.astype(jnp.float32)
    weight_grad = lax.fori_loop(0, N_SEQ, add_block, jnp.zeros((HEAD_COUNT * P_SIZE, D), jnp.float32)).astype(jnp.bfloat16)
    inputs = (log_decay.reshape(N_SEQ, L_DEV, HEAD_COUNT), scan_grad.reshape(N_SEQ, L_DEV, HEAD_COUNT, P_SIZE), step_size.reshape(N_SEQ, L_DEV, HEAD_COUNT), input_map.reshape(N_SEQ, L_DEV, G, N), output_map.reshape(N_SEQ, L_DEV, G, N))
    initial = jnp.zeros((HEAD_COUNT, P_SIZE, N), jnp.float32)
    final_state, results = lax.scan(partial(block_grads, skip_gain), initial, inputs, reverse=True)
    input_grad = results.reshape(TOKEN_COUNT, HEAD_COUNT * P_SIZE)
    return (input_grad, gate_grad, weight_grad)
```

```python
import math

import jax
import jax.numpy as jnp
from jax import lax
from jax.sharding import PartitionSpec as P

HEAD_COUNT = 128
G = 4
SUB = 128

f32 = jnp.float32
bf16 = jnp.bfloat16
highest = lax.Precision.HIGHEST


def gate_terms(gate_input, scan_output):
    gate_value = gate_input.astype(f32)
    sig = jax.nn.sigmoid(gate_value)
    silu = gate_value * sig
    saved = scan_output.astype(f32)
    slope = saved * sig * (1.0 + gate_value * (1.0 - sig))
    gated = (saved * silu).astype(bf16)
    return silu, slope, gated


def spread_heads(values, width):
    heads = values.shape[1]
    owner = jnp.arange(heads * width) // width
    expand = (owner[None, :] == jnp.arange(heads)[:, None]).astype(f32)
    return jnp.dot(values, expand, precision=highest, preferred_element_type=f32)


def scan_pieces(scan_grad, cumulative, in_group, out_group):
    length, heads = cumulative.shape
    width = scan_grad.shape[1] // heads
    chunks = length // SUB
    grad_float = scan_grad.astype(f32)
    weighted = (grad_float * spread_heads(jnp.exp(cumulative), width)).astype(bf16)
    local_state = jnp.einsum("tk,tn->kn", weighted, out_group, preferred_element_type=f32)

    ends = cumulative[SUB - 1 :: SUB]
    b_c = in_group.reshape(chunks, SUB, -1)
    c_c = out_group.reshape(chunks, SUB, -1)
    scores = jnp.einsum("ctn,csn->cts", b_c, c_c, preferred_element_type=f32)
    cum_c = cumulative.reshape(chunks, SUB, heads).transpose(0, 2, 1)
    spread = cum_c[:, :, None, :] - cum_c[:, :, :, None]
    pos = jnp.arange(SUB)
    mask = pos[:, None] <= pos[None, :]
    factor = jnp.where(mask, jnp.exp(jnp.minimum(spread, 0.0)), 0.0)
    weights = (scores[:, None] * factor).astype(bf16)
    grads = scan_grad.reshape(chunks, SUB, heads, width)
    inside = jnp.einsum("chts,cshp->cthp", weights, grads, preferred_element_type=f32)
    inside = inside.reshape(length, heads * width)
    state = None
    later = [jnp.zeros((SUB, heads * width), f32)]
    for j in range(chunks - 2, -1, -1):
        rows = slice((j + 1) * SUB, (j + 2) * SUB)
        decay = spread_heads(jnp.exp(cumulative[rows] - ends[j][None]), width)
        fresh = jnp.einsum(
            "tn,tk->nk",
            out_group[rows],
            (grad_float[rows] * decay).astype(bf16),
            preferred_element_type=f32,
        )
        state = fresh if state is None else fresh + decay[-1][None] * state
        seen = jnp.dot(
            in_group[j * SUB : (j + 1) * SUB], state.astype(bf16), preferred_element_type=f32
        )
        tail = spread_heads(jnp.exp(ends[j][None] - cumulative[j * SUB : (j + 1) * SUB]), width)
        later.insert(0, seen * tail)
    return local_state, inside + jnp.concatenate(later, axis=0)


def group_maps(input_map, output_map, heads_here):
    index = lax.axis_index("head") * heads_here // (HEAD_COUNT // G)
    pick = lambda m: lax.dynamic_index_in_dim(m, index, 1, keepdims=False)
    return pick(input_map), pick(output_map)


def finish(inside, carried, scan_grad, cumulative, in_group, step_size, skip_gain):
    heads = cumulative.shape[1]
    width = scan_grad.shape[1] // heads
    seen = jnp.einsum("tn,kn->tk", in_group, carried.astype(bf16), preferred_element_type=f32)
    tail = spread_heads(jnp.exp(cumulative[-1:] - cumulative), width)
    return (
        spread_heads(step_size, width) * (inside + tail * seen)
        + jnp.repeat(skip_gain, width)[None] * scan_grad.astype(f32)
    ).astype(bf16)


def general(
    out_grad,
    out_weight,
    gate_input,
    scan_output,
    step_size,
    log_decay,
    input_map,
    output_map,
    skip_gain,
):
    length = out_grad.shape[0]
    heads_here = log_decay.shape[1]
    n_seq = lax.axis_size("seq")
    width = gate_input.shape[1] // heads_here
    cols = out_weight.shape[1]
    silu, slope, gated = gate_terms(gate_input, scan_output)
    mine = lax.dynamic_slice_in_dim(out_grad, lax.axis_index("head") * cols, cols, 1)
    row_panel = lax.all_to_all(out_weight, "head", split_axis=0, concat_axis=1, tiled=True)
    upstream = jnp.einsum("td,kd->tk", out_grad, row_panel, preferred_element_type=f32)
    gate_grad = (upstream * slope).astype(bf16)
    scan_grad = (upstream * silu).astype(bf16)
    in_group, out_group = group_maps(input_map, output_map, heads_here)
    cumulative = jnp.cumsum(log_decay, axis=0)
    local_state, inside = scan_pieces(scan_grad, cumulative, in_group, out_group)
    decay_all = jnp.repeat(jnp.exp(cumulative[-1]), width)[:, None]

    def relay_turn(_, carried_in):
        outgoing = (local_state + decay_all * carried_in).astype(bf16)
        route = [(i + 1, i) for i in range(n_seq - 1)]
        return lax.ppermute(outgoing, "seq", route).astype(f32)

    carried = lax.fori_loop(0, n_seq - 1, relay_turn, jnp.zeros_like(local_state))
    input_grad = finish(inside, carried, scan_grad, cumulative, in_group, step_size, skip_gain)
    gated_all = lax.all_gather(gated, "head", axis=1, tiled=True)
    part = jnp.einsum("tk,td->kd", gated_all, mine, preferred_element_type=f32)
    part = (part * (1.0 / math.sqrt(length * n_seq))).astype(bf16)
    return input_grad, gate_grad, lax.psum(part, "seq")


def send(block, move, n_seq, n_head):
    route = []
    for s in range(n_seq):
        for h in range(n_head):
            to = move(s, h)
            if to is not None:
                route.append((s * n_head + h, to[0] * n_head + to[1]))
    return lax.ppermute(block, ("seq", "head"), route)


def routed(
    out_grad,
    out_weight,
    gate_input,
    scan_output,
    step_size,
    log_decay,
    input_map,
    output_map,
    skip_gain,
):
    length = out_grad.shape[0]
    heads_here = log_decay.shape[1]
    width = gate_input.shape[1] // heads_here
    cols = out_weight.shape[1]
    n_seq, n_head = lax.axis_size("seq"), lax.axis_size("head")
    nz = n_head // 2
    s_id, h_id = lax.axis_index("seq"), lax.axis_index("head")
    z_id, core = h_id // 2, h_id % 2

    def go(block, move):
        return send(block, move, n_seq, n_head)

    def over_x(block):
        return go(block, lambda s, h: (s ^ 1, h))

    def over_y(block):
        return go(block, lambda s, h: (s ^ 2, h))

    def over_core(block):
        return go(block, lambda s, h: (s, h ^ 1))

    def up(block, first=0):
        return go(block, lambda s, h: (s, h + 2) if first <= h // 2 < nz - 1 else None)

    def down(block, last=nz - 1):
        return go(block, lambda s, h: (s, h - 2) if 0 < h // 2 <= last else None)

    silu, slope, gated = gate_terms(gate_input, scan_output)
    mine = lax.dynamic_slice_in_dim(out_grad, h_id * cols, cols, 1)

    half = length // 2

    def in_plane(block):
        from_x, from_y = over_x(block), over_y(block)
        top, bottom = over_y(from_x[:half]), over_x(from_y[half:])
        return jnp.concatenate([block, from_x, from_y, top, bottom], axis=0)

    def segment(k):
        row = ((z_id + k) % nz) * 2

        def product(c):
            rows = lax.dynamic_slice_in_dim(out_weight, (row + c) * cols, cols, 0)
            return jnp.einsum("td,kd->tk", mine, rows, preferred_element_type=f32)

        other = over_core(product(1 - core).astype(bf16))
        return product(core) + other.astype(f32)

    segments = {}
    for t in range(nz - 1):
        for k in (nz - 1 - t, 1 + t):
            if k not in segments:
                segments[k] = segment(k)
    segments[0] = segment(0)

    from_below = from_above = None
    for t in range(nz - 1):
        rising, falling = segments[nz - 1 - t], segments[1 + t]
        if t:
            rising = rising + from_below.astype(f32)
            falling = falling + from_above.astype(f32)
        from_below = go(
            rising.astype(bf16),
            lambda s, h: (s, h + 2) if h // 2 <= t and h // 2 < nz - 1 else None,
        )
        from_above = go(
            falling.astype(bf16),
            lambda s, h: (s, h - 2) if h // 2 >= nz - 1 - t and h // 2 > 0 else None,
        )
    upstream = segments[0] + from_below.astype(f32) + from_above.astype(f32)

    below, above = {0: gated}, {0: gated}
    for j in range(1, nz):
        below[j] = up(below[j - 1], j - 1)
        above[j] = down(above[j - 1], nz - j)
    arrivals = [(gated, z_id)]
    for j in range(1, nz):
        takes = []
        for z in range(nz):
            order = sorted(
                [("a", d, z + d) for d in range(1, nz - z)]
                + [("b", d, z - d) for d in range(1, z + 1)],
                key=lambda e: (e[1], e[0]),
            )
            takes.append(order[j - 1])
        block, plane = None, jnp.int32(0)
        for z in range(nz):
            side, d, p = takes[z]
            held = above[d] if side == "a" else below[d]
            block = held if block is None else jnp.where(z_id == z, held, block)
            plane = jnp.where(z_id == z, p, plane)
        arrivals.append((block, plane))

    gate_grad = (upstream * slope).astype(bf16)
    scan_grad = (upstream * silu).astype(bf16)
    in_group, out_group = group_maps(input_map, output_map, heads_here)
    cumulative = jnp.cumsum(log_decay, axis=0)
    total = cumulative[-1:]
    total_x = over_x(total)
    local_state, inside = scan_pieces(scan_grad, cumulative, in_group, out_group)

    def column(v):
        return jnp.repeat(jnp.exp(v[0]), width)[:, None]

    own = local_state
    from_x = over_x(own.astype(bf16)).astype(f32)
    pair = jnp.where(s_id == 2, own + column(total) * from_x, from_x + column(total_x) * own)
    from_y = over_y(pair.astype(bf16)).astype(f32)
    carried = jnp.where(
        s_id == 0,
        from_x + column(total_x) * from_y,
        jnp.where(s_id == 1, from_y, jnp.where(s_id == 2, from_x, 0.0)),
    )
    input_grad = finish(inside, carried, scan_grad, cumulative, in_group, step_size, skip_gain)

    grad_scale = 1.0 / math.sqrt(length * n_seq)
    grads = in_plane(mine)
    weight_grad = jnp.zeros((n_head * cols, cols), bf16)
    for block, plane in arrivals:
        rows = in_plane(block)
        for whose, held in ((core, rows), (1 - core, over_core(rows))):
            part = jnp.einsum("tk,td->kd", held, grads, preferred_element_type=f32) * grad_scale
            weight_grad = lax.dynamic_update_slice_in_dim(
                weight_grad, part.astype(bf16), (plane * 2 + whose) * cols, 0
            )
    return input_grad, gate_grad, weight_grad


def solution(mesh):
    in_specs = (
        P("seq", None),
        P(None, "head"),
        P("seq", "head"),
        P("seq", "head"),
        P("seq", "head"),
        P("seq", "head"),
        P("seq", None, None),
        P("seq", None, None),
        P("head"),
    )
    out_specs = (P("seq", "head"), P("seq", "head"), P(None, "head"))
    small = mesh.shape["seq"] == 4 and mesh.shape["head"] == 8
    return jax.shard_map(
        routed if small else general,
        mesh=mesh,
        in_specs=in_specs,
        out_specs=out_specs,
        check_vma=False,
    )
```

```python
import math

import jax
import jax.numpy as jnp
from jax import lax
from jax.experimental import pallas as pl
from jax.experimental.pallas import tpu as pltpu
from jax.sharding import PartitionSpec as P

HEAD_COUNT = 128
G = 4
SUB = 128

f32 = jnp.float32
bf16 = jnp.bfloat16
highest = lax.Precision.HIGHEST
MESH = pl.DeviceIdType.MESH


def gate_terms(gate_input, scan_output):
    gate_value = gate_input.astype(f32)
    sig = jax.nn.sigmoid(gate_value)
    silu = gate_value * sig
    saved = scan_output.astype(f32)
    slope = saved * sig * (1.0 + gate_value * (1.0 - sig))
    gated = (saved * silu).astype(bf16)
    return silu, slope, gated


def spread_heads(values, width):
    heads = values.shape[1]
    owner = jnp.arange(heads * width) // width
    expand = (owner[None, :] == jnp.arange(heads)[:, None]).astype(f32)
    return jnp.dot(values, expand, precision=highest, preferred_element_type=f32)


def scan_pieces(scan_grad, cumulative, in_group, out_group):
    length, heads = cumulative.shape
    width = scan_grad.shape[1] // heads
    chunks = length // SUB
    grad_float = scan_grad.astype(f32)
    weighted = (grad_float * spread_heads(jnp.exp(cumulative), width)).astype(bf16)
    local_state = jnp.einsum("tk,tn->kn", weighted, out_group, preferred_element_type=f32)

    ends = cumulative[SUB - 1 :: SUB]
    b_c = in_group.reshape(chunks, SUB, -1)
    c_c = out_group.reshape(chunks, SUB, -1)
    scores = jnp.einsum("ctn,csn->cts", b_c, c_c, preferred_element_type=f32)
    cum_c = cumulative.reshape(chunks, SUB, heads).transpose(0, 2, 1)
    spread = cum_c[:, :, None, :] - cum_c[:, :, :, None]
    pos = jnp.arange(SUB)
    mask = pos[:, None] <= pos[None, :]
    factor = jnp.where(mask, jnp.exp(jnp.minimum(spread, 0.0)), 0.0)
    weights = (scores[:, None] * factor).astype(bf16)
    grads = scan_grad.reshape(chunks, SUB, heads, width)
    inside = jnp.einsum("chts,cshp->cthp", weights, grads, preferred_element_type=f32)
    inside = inside.reshape(length, heads * width)
    state = None
    later = [jnp.zeros((SUB, heads * width), f32)]
    for j in range(chunks - 2, -1, -1):
        rows = slice((j + 1) * SUB, (j + 2) * SUB)
        decay = spread_heads(jnp.exp(cumulative[rows] - ends[j][None]), width)
        fresh = jnp.einsum(
            "tn,tk->nk",
            out_group[rows],
            (grad_float[rows] * decay).astype(bf16),
            preferred_element_type=f32,
        )
        state = fresh if state is None else fresh + decay[-1][None] * state
        seen = jnp.dot(
            in_group[j * SUB : (j + 1) * SUB], state.astype(bf16), preferred_element_type=f32
        )
        tail = spread_heads(jnp.exp(ends[j][None] - cumulative[j * SUB : (j + 1) * SUB]), width)
        later.insert(0, seen * tail)
    return local_state, inside + jnp.concatenate(later, axis=0)


def group_maps(input_map, output_map, heads_here):
    index = lax.axis_index("head") * heads_here // (HEAD_COUNT // G)
    pick = lambda m: lax.dynamic_index_in_dim(m, index, 1, keepdims=False)
    return pick(input_map), pick(output_map)


def finish(inside, carried, scan_grad, cumulative, in_group, step_size, skip_gain):
    heads = cumulative.shape[1]
    width = scan_grad.shape[1] // heads
    seen = jnp.einsum("tn,kn->tk", in_group, carried.astype(bf16), preferred_element_type=f32)
    tail = spread_heads(jnp.exp(cumulative[-1:] - cumulative), width)
    return (
        spread_heads(step_size, width) * (inside + tail * seen)
        + jnp.repeat(skip_gain, width)[None] * scan_grad.astype(f32)
    ).astype(bf16)


def general(
    out_grad,
    out_weight,
    gate_input,
    scan_output,
    step_size,
    log_decay,
    input_map,
    output_map,
    skip_gain,
):
    length = out_grad.shape[0]
    heads_here = log_decay.shape[1]
    n_seq = lax.axis_size("seq")
    width = gate_input.shape[1] // heads_here
    cols = out_weight.shape[1]
    silu, slope, gated = gate_terms(gate_input, scan_output)
    mine = lax.dynamic_slice_in_dim(out_grad, lax.axis_index("head") * cols, cols, 1)
    row_panel = lax.all_to_all(out_weight, "head", split_axis=0, concat_axis=1, tiled=True)
    upstream = jnp.einsum("td,kd->tk", out_grad, row_panel, preferred_element_type=f32)
    gate_grad = (upstream * slope).astype(bf16)
    scan_grad = (upstream * silu).astype(bf16)
    in_group, out_group = group_maps(input_map, output_map, heads_here)
    cumulative = jnp.cumsum(log_decay, axis=0)
    local_state, inside = scan_pieces(scan_grad, cumulative, in_group, out_group)
    decay_all = jnp.repeat(jnp.exp(cumulative[-1]), width)[:, None]

    def relay_turn(_, carried_in):
        outgoing = (local_state + decay_all * carried_in).astype(bf16)
        route = [(i + 1, i) for i in range(n_seq - 1)]
        return lax.ppermute(outgoing, "seq", route).astype(f32)

    carried = lax.fori_loop(0, n_seq - 1, relay_turn, jnp.zeros_like(local_state))
    input_grad = finish(inside, carried, scan_grad, cumulative, in_group, step_size, skip_gain)
    gated_all = lax.all_gather(gated, "head", axis=1, tiled=True)
    part = jnp.einsum("tk,td->kd", gated_all, mine, preferred_element_type=f32)
    part = (part * (1.0 / math.sqrt(length * n_seq))).astype(bf16)
    return input_grad, gate_grad, lax.psum(part, "seq")


def mirror(at, upper):
    return at + upper * (3 - 2 * at)


def exchange(
    out_grad,
    out_weight,
    gated_t,
    gate_input,
    scan_output,
    in_group,
    out_group_t,
    factors,
    cumul,
    cumul_t,
    expand,
    skip,
    weight_grad,
    gate_grad,
    input_grad,
    cls,
    og,
    wbuf,
    xsend,
    xrecv,
    xsum,
    rs,
    st_own,
    st_x,
    st_pair,
    st_y,
    total,
    total_x,
    inside,
    state,
    local_sem,
    w_sem,
    xs,
    xr,
    rss,
    rsr,
    zs,
    zr,
    es,
    er,
    bs,
    br,
    cs,
    cr,
    ks,
    kr,
    ts,
    tr,
    ol,
    os_,
    or_,
):
    cols, length = gated_t.shape
    tile = min(256, cols)
    tiles = cols // tile
    s, h = lax.axis_index("seq"), lax.axis_index("head")
    z, core = lax.div(h, 2), lax.rem(h, 2)
    upper = lax.div(z, 2)
    zz = z + upper * (3 - 2 * z)
    inner, end = zz == 1, zz == 0
    mate = h + 1 - 2 * core
    dev_core = (s, mate)
    dev_x = (s + 1 - 2 * lax.rem(s, 2), h)
    dev_y = (lax.rem(s + 2, 4), h)
    inward = mirror(zz + 1, upper)
    dev_in = (s, inward * 2 + core)
    dev_out = (s, mirror(0, upper) * 2 + core)
    seg = [mirror(3, upper), mirror(2, upper), mirror(1 - zz, upper), z]
    plane = [z, inward, mirror(2 - 2 * zz, upper), mirror(3, upper)]

    def remote(src, dst, ssem, rsem, dev):
        return pltpu.make_async_remote_copy(
            src_ref=src, dst_ref=dst, send_sem=ssem, recv_sem=rsem, device_id=dev, device_id_type=MESH
        )

    heads = cumul.shape[1]
    width = cols // heads
    sub = length // 4

    def spread(values):
        return jnp.dot(values, expand[...], precision=highest, preferred_element_type=f32)

    def own_cols(part, sem):
        who = h if part == 0 else mate
        return pltpu.make_async_copy(
            out_grad.at[:, pl.ds(pl.multiple_of(who * cols, cols), cols)],
            og.at[pl.ds(0, length), pl.ds(part * cols, cols)],
            local_sem.at[sem],
        )

    def w_load(i):
        who = (1 - core) if i % 2 == 0 else core
        row = pl.multiple_of((seg[i // 2] * 2 + who) * cols, cols)
        return pltpu.make_async_copy(
            out_weight.at[pl.ds(row, cols), :], wbuf.at[i % 2], w_sem.at[i % 2]
        )

    own_cols(0, 0).start()
    own_cols(1, 1).start()
    w_load(0).start()
    w_load(1).start()

    barrier = pltpu.get_barrier_semaphore()
    for dev in (dev_core, dev_x, dev_y, dev_in):
        pl.semaphore_signal(barrier, inc=1, device_id=dev, device_id_type=MESH)

    @pl.when(inner)
    def _():
        pl.semaphore_signal(barrier, inc=1, device_id=dev_out, device_id_type=MESH)

    @pl.when(inner)
    def _():
        pl.semaphore_wait(barrier, 5)

    @pl.when(end)
    def _():
        pl.semaphore_wait(barrier, 4)

    def token(b):
        return pl.ds(b * length, length)

    def z_own(k):
        return remote(
            gated_t, cls.at[z, :, token(0)], zs.at[k], zr.at[z], dev_in if k == 0 else dev_out
        )

    def z_pass(j):
        block = cls.at[plane[j], :, token(0)]
        return remote(block, block, zs.at[j + 1], zr.at[plane[j]], dev_in if j == 2 else dev_out)

    def z_arrive(j):
        block = cls.at[plane[j], :, token(0)]
        remote(block, block, zs.at[0], zr.at[plane[j]], dev_in).wait_recv()

    quarter = cols // 4
    kept = cols - quarter

    def extra(j):
        return cls.at[plane[j], pl.ds(kept, quarter), pl.ds(length, 3 * length)]

    def e_own(k):
        block = extra(0)
        return remote(block, block, es.at[k], er.at[z], dev_in if k == 0 else dev_out)

    def e_pass(j):
        block = extra(j)
        return remote(block, block, es.at[j + 1], er.at[plane[j]], dev_in if j == 2 else dev_out)

    def e_arrive(j):
        block = extra(j)
        remote(block, block, es.at[0], er.at[plane[j]], dev_in).wait_recv()

    def b_copy(j, kind):
        p = plane[j]
        count = cols if j == 0 else kept
        rows = pl.ds(0, count)
        if kind < 2:
            src = gated_t.at[rows, :] if j == 0 else cls.at[p, rows, token(0)]
            dst = cls.at[p, rows, token(kind + 1)]
            dev = dev_x if kind == 0 else dev_y
        else:
            rows = pl.ds(0, count // 2) if kind == 2 else pl.ds(count // 2, count // 2)
            src = cls.at[p, rows, token(1 if kind == 2 else 2)]
            dst = cls.at[p, rows, token(3)]
            dev = dev_y if kind == 2 else dev_x
        return remote(src, dst, bs.at[j, kind], br.at[j, kind], dev)

    def b_first(j):
        b_copy(j, 0).start()
        b_copy(j, 1).start()

    def b_second(j):
        b_copy(j, 0).wait_recv()
        b_copy(j, 2).start()
        b_copy(j, 1).wait_recv()
        b_copy(j, 3).start()

    def b_last(j):
        b_copy(j, 2).wait_recv()
        b_copy(j, 3).wait_recv()

    hl = length // 2
    c_rows = [
        pl.ds(length, length),
        pl.ds(2 * length, length),
        pl.ds(3 * length, hl),
        pl.ds(3 * length + hl, hl),
    ]

    def c_copy(kind):
        src_rows = [pl.ds(0, length), pl.ds(0, length), pl.ds(length, hl), pl.ds(2 * length + hl, hl)]
        dev = dev_x if kind in (0, 3) else dev_y
        mine = pl.ds(0, cols)
        return remote(
            og.at[src_rows[kind], mine], og.at[c_rows[kind], mine], cs.at[kind], cr.at[kind], dev
        )

    def k_copy(kind):
        return remote(
            og.at[c_rows[kind], pl.ds(0, cols)],
            og.at[c_rows[kind], pl.ds(cols, cols)],
            ks.at[kind],
            kr.at[kind],
            dev_core,
        )

    b_first(0)

    z_own(0).start()

    @pl.when(inner)
    def _():
        z_own(1).start()

    own_cols(0, 0).wait()
    own_cols(1, 1).wait()
    c_copy(0).start()
    c_copy(1).start()
    total[...] = spread(jnp.broadcast_to(factors[0, length - 1 :, :], (8, heads)))
    total_copy = remote(total, total_x, ts.at[2], tr.at[2], dev_x)
    total_copy.start()

    def product(i, dst):
        w_load(i).wait()

        def step(r, _):
            lanes = pl.ds(pl.multiple_of(r * tile, tile), tile)
            part = lax.dot_general(
                og[pl.ds(0, length), pl.ds(0, cols)],
                wbuf[i % 2, lanes, :],
                (((1,), (1,)), ((), ())),
                preferred_element_type=f32,
            )
            dst[:, lanes] = part.astype(bf16)
            return 0

        lax.fori_loop(0, tiles, step, 0)
        if i + 2 < 8:
            w_load(i + 2).start()

    def x_copy(n):
        return remote(xsend.at[n % 2], xrecv.at[n], xs.at[n % 2], xr.at[n], dev_core)

    rows_at_once = min(64, length)

    def by_rows(body):
        def step(r, _):
            body(pl.ds(pl.multiple_of(r * rows_at_once, rows_at_once), rows_at_once))
            return 0

        lax.fori_loop(0, length // rows_at_once, step, 0)

    def add_into(n, other):
        def body(rows):
            xsum[n, rows, :] = (xsum[n, rows, :].astype(f32) + other[rows, :].astype(f32)).astype(bf16)

        by_rows(body)

    def rs_end(n):
        return remote(xsum.at[n], rs.at[n], rss.at[n], rsr.at[n], dev_in)

    def rs_inner(n):
        dst, dev = [(3, dev_in), (4, dev_in), (2, dev_out)][n]
        return remote(xsum.at[n], rs.at[dst], rss.at[n], rsr.at[dst], dev)

    def rs_arrive(slot):
        remote(rs.at[slot], rs.at[slot], rss.at[0], rsr.at[slot], dev_in).wait_recv()

    for n in range(4):
        if n >= 2:
            x_copy(n - 2).wait_send()
        product(2 * n, xsend.at[n % 2])
        x_copy(n).start()
        product(2 * n + 1, xsum.at[n])
        if n:
            x_copy(n - 1).wait_recv()
            add_into(n - 1, xrecv.at[n - 1])

            @pl.when(end)
            def _():
                rs_end(n - 1).start()

    x_copy(3).wait_recv()
    x_copy(2).wait_send()
    x_copy(3).wait_send()

    def place(r, _):
        rows = pl.ds(pl.multiple_of(r * tile, tile), tile)
        cls[z, rows, token(0)] = gated_t[rows, :]
        return 0

    lax.fori_loop(0, tiles, place, 0)

    z_arrive(1)
    b_first(1)

    @pl.when(inner)
    def _():
        z_pass(1).start()
        z_arrive(2)
        z_pass(2).start()

    b_second(0)

    @pl.when(inner)
    def _():
        rs_arrive(0)
        add_into(0, rs.at[0])
        rs_inner(0).start()

    c_copy(0).wait_recv()
    c_copy(2).start()
    k_copy(0).start()
    c_copy(1).wait_recv()
    c_copy(3).start()
    k_copy(1).start()

    @pl.when(inner)
    def _():
        z_arrive(3)
        z_pass(3).start()
        rs_arrive(1)
        add_into(1, rs.at[1])
        rs_inner(1).start()
        rs_arrive(3)
        add_into(2, rs.at[3])
        rs_inner(2).start()

    @pl.when(end)
    def _():
        z_arrive(2)

    b_first(2)
    b_last(0)
    e_own(0).start()

    @pl.when(inner)
    def _():
        e_own(1).start()

    c_copy(2).wait_recv()
    k_copy(2).start()
    c_copy(3).wait_recv()
    k_copy(3).start()
    for kind in range(4):
        k_copy(kind).wait_recv()

    grad_scale = 1.0 / math.sqrt(length * 4)
    wide = min(512, cols)

    def out_local(j, r):
        row = pl.multiple_of((plane[j] * 2 + core) * cols + r * tile, tile)
        rows = pl.ds(pl.multiple_of(r * tile, tile), tile)
        return pltpu.make_async_copy(
            wbuf.at[0, rows, :], weight_grad.at[pl.ds(row, tile), :], ol.at[r]
        )

    def out_remote(j, r):
        row = pl.multiple_of((plane[j] * 2 + core) * cols + r * tile, tile)
        rows = pl.ds(pl.multiple_of(r * tile, tile), tile)
        return remote(
            wbuf.at[1, rows, :], weight_grad.at[pl.ds(row, tile), :], os_.at[r], or_.at[j, r], dev_core
        )

    def out_arrive(j, r):
        row = pl.multiple_of((plane[j] * 2 + 1 - core) * cols + r * tile, tile)
        there = weight_grad.at[pl.ds(row, tile), :]
        remote(there, there, os_.at[r], or_.at[j, r], dev_core).wait_recv()

    def rows_of(j):
        def step(r, _):
            rows = pl.ds(pl.multiple_of(r * tile, tile), tile)
            if j:
                out_local(j - 1, r).wait()
                out_remote(j - 1, r).wait_send()
            for n in range(2 * cols // wide):
                part = jnp.dot(
                    cls[plane[j], rows, :],
                    og[:, pl.ds(n * wide, wide)],
                    preferred_element_type=f32,
                )
                at = n * wide
                wbuf[at // cols, rows, pl.ds(at % cols, wide)] = (part * grad_scale).astype(bf16)
            out_local(j, r).start()
            out_remote(j, r).start()
            return 0

        lax.fori_loop(0, tiles, step, 0)

    rows_of(0)

    rs_arrive(2)

    @pl.when(inner)
    def _():
        rs_arrive(4)

    def top(rows):
        up = xsum[3, rows, :].astype(f32) + xrecv[3, rows, :].astype(f32) + rs[2, rows, :].astype(f32)
        up = jnp.where(inner, up + rs[4, rows, :].astype(f32), up)
        gate = gate_input[rows, :].astype(f32)
        sig = 1.0 / (1.0 + jnp.exp(-gate))
        saved = scan_output[rows, :].astype(f32)
        gate_grad[rows, :] = (up * saved * sig * (1.0 + gate * (1.0 - sig))).astype(bf16)
        grad = (up * (gate * sig)).astype(bf16)
        xsend[1, rows, :] = grad
        xsend[0, rows, :] = (grad.astype(f32) * spread(factors[0, rows, :])).astype(bf16)

    by_rows(top)
    st_own[...] = jnp.dot(out_group_t[...], xsend[0], preferred_element_type=f32).astype(bf16)
    hop_x = remote(st_own, st_x, ts.at[0], tr.at[0], dev_x)
    hop_x.start()

    def inside_of(j):
        rows = pl.ds(j * sub, sub)
        scores = jnp.dot(
            in_group[rows, :], out_group_t[:, j * sub : (j + 1) * sub], preferred_element_type=f32
        )
        at_t = lax.broadcasted_iota(jnp.int32, (sub, sub), 0)
        at_s = lax.broadcasted_iota(jnp.int32, (sub, sub), 1)
        scores = jnp.where(at_t <= at_s, scores, 0.0)
        left = lax.broadcasted_iota(jnp.int32, (sub, 2 * width), 1) < width
        for pair in range(heads // 2):
            lanes = pl.ds(pair * 2 * width, 2 * width)
            grads = xsend[1, rows, lanes]
            sums = []
            for head in (2 * pair, 2 * pair + 1):
                ahead = cumul_t[head : head + 1, j * sub : (j + 1) * sub] - cumul[rows, head : head + 1]
                weights = (scores * jnp.exp(jnp.minimum(ahead, 0.0))).astype(bf16)
                sums.append(jnp.dot(weights, grads, preferred_element_type=f32))
            inside[rows, lanes] = jnp.where(left, sums[0], sums[1])
        if j < 3:
            seen = jnp.dot(in_group[rows, :], state[...].astype(bf16), preferred_element_type=f32)
            inside[rows, :] += seen * spread(factors[2, rows, :])
        if j:
            decay = spread(factors[1, rows, :])
            fresh = jnp.dot(
                out_group_t[:, j * sub : (j + 1) * sub],
                (xsend[1, rows, :].astype(f32) * decay).astype(bf16),
                preferred_element_type=f32,
            )
            state[...] = fresh if j == 3 else fresh + decay[sub - 1 :, :] * state[...]

    def finish_rows(j):
        rows = pl.ds(j * sub, sub)
        seen = jnp.dot(in_group[rows, :], st_own[...], preferred_element_type=f32)
        grad = xsend[1, rows, :].astype(f32)
        input_grad[rows, :] = (
            spread(factors[4, rows, :]) * (inside[rows, :] + spread(factors[3, rows, :]) * seen)
            + skip[0:1, :] * grad
        ).astype(bf16)

    b_second(1)

    @pl.when(end)
    def _():
        z_arrive(3)

    b_first(3)

    @pl.when(inner)
    def _():
        e_arrive(1)
        e_pass(1).start()
        e_arrive(2)
        e_pass(2).start()

    inside_of(3)
    inside_of(2)
    total_copy.wait_recv()
    hop_x.wait_recv()
    hop_y = remote(st_pair, st_y, ts.at[1], tr.at[1], dev_y)
    mine, theirs = st_own[...].astype(f32), st_x[...].astype(f32)
    st_pair[...] = jnp.where(
        s == 2, mine + total[0:1, :] * theirs, theirs + total_x[0:1, :] * mine
    ).astype(bf16)

    @pl.when(s >= 2)
    def _():
        hop_y.start()

    b_second(2)

    @pl.when(end)
    def _():
        e_arrive(1)

    b_last(1)
    rows_of(1)

    @pl.when(inner)
    def _():
        e_arrive(3)
        e_pass(3).start()

    hop_x.wait_send()

    @pl.when(s < 2)
    def _():
        hop_y.wait_recv()
        later = st_y[...].astype(f32)
        st_own[...] = jnp.where(
            s == 0, st_x[...].astype(f32) + total_x[0:1, :] * later, later
        ).astype(bf16)

    @pl.when(s >= 2)
    def _():
        st_own[...] = jnp.where(s == 2, st_x[...].astype(f32), 0.0).astype(bf16)

    inside_of(1)
    inside_of(0)
    b_second(3)

    @pl.when(end)
    def _():
        e_arrive(2)

    b_last(2)
    rows_of(2)
    for j in range(4):
        finish_rows(j)
    b_last(3)

    @pl.when(end)
    def _():
        e_arrive(3)

    rows_of(3)

    for j in range(4):
        for kind in range(4):
            b_copy(j, kind).wait_send()
    for kind in range(4):
        c_copy(kind).wait_send()
        k_copy(kind).wait_send()
    total_copy.wait_send()

    @pl.when(s >= 2)
    def _():
        hop_y.wait_send()

    z_own(0).wait_send()
    e_own(0).wait_send()
    for n in range(3):
        rs_end(n).wait_send()

    @pl.when(inner)
    def _():
        z_own(1).wait_send()
        e_own(1).wait_send()
        for j in (1, 2, 3):
            z_pass(j).wait_send()
            e_pass(j).wait_send()

    def drain(r, _):
        out_local(3, r).wait()
        out_remote(3, r).wait_send()
        for j in range(4):
            out_arrive(j, r)
        return 0

    lax.fori_loop(0, tiles, drain, 0)


def scan_factors(cumul, step_size):
    length = cumul.shape[0]
    sub = length // 4
    ends = cumul[sub - 1 :: sub]
    zero = jnp.zeros_like(ends[:1])
    before = jnp.repeat(jnp.concatenate([zero, ends[:-1]]), sub, axis=0)
    after = jnp.repeat(ends, sub, axis=0)
    fades = [cumul, cumul - before, after - cumul, ends[-1:] - cumul]
    return jnp.stack([jnp.exp(f) for f in fades] + [step_size])


def call_exchange(
    out_grad, out_weight, gated_t, gate_input, scan_output, in_group, out_group_t, factors, cumul, skip
):
    cols, length = gated_t.shape
    state = out_group_t.shape[0]
    heads = cumul.shape[1]
    tiles = cols // min(256, cols)
    dma = pltpu.SemaphoreType.DMA
    hbm = pl.BlockSpec(memory_space=pl.ANY)
    vmem = pl.BlockSpec(memory_space=pltpu.VMEM)
    owner = jnp.arange(cols) // (cols // heads)
    expand = (owner[None, :] == jnp.arange(heads)[:, None]).astype(f32)
    skip = jnp.broadcast_to(jnp.repeat(skip, cols // heads)[None], (8, cols))
    return pl.pallas_call(
        exchange,
        out_shape=(
            jax.ShapeDtypeStruct(out_weight.shape, bf16),
            jax.ShapeDtypeStruct((length, cols), bf16),
            jax.ShapeDtypeStruct((length, cols), bf16),
        ),
        in_specs=[hbm, hbm] + [vmem] * 10,
        out_specs=(hbm, vmem, vmem),
        scratch_shapes=[
            pltpu.VMEM((4, cols, 4 * length), bf16),
            pltpu.VMEM((4 * length, 2 * cols), bf16),
            pltpu.VMEM((2, cols, cols), bf16),
            pltpu.VMEM((2, length, cols), bf16),
            pltpu.VMEM((4, length, cols), bf16),
            pltpu.VMEM((4, length, cols), bf16),
            pltpu.VMEM((5, length, cols), bf16),
            pltpu.VMEM((state, cols), bf16),
            pltpu.VMEM((state, cols), bf16),
            pltpu.VMEM((state, cols), bf16),
            pltpu.VMEM((state, cols), bf16),
            pltpu.VMEM((8, cols), f32),
            pltpu.VMEM((8, cols), f32),
            pltpu.VMEM((length, cols), f32),
            pltpu.VMEM((state, cols), f32),
            dma((2,)),
            dma((2,)),
            dma((2,)),
            dma((4,)),
            dma((3,)),
            dma((5,)),
            dma((5,)),
            dma((4,)),
            dma((5,)),
            dma((4,)),
            dma((4, 4)),
            dma((4, 4)),
            dma((4,)),
            dma((4,)),
            dma((4,)),
            dma((4,)),
            dma((3,)),
            dma((3,)),
            dma((tiles,)),
            dma((tiles,)),
            dma((4, tiles)),
        ],
        compiler_params=pltpu.CompilerParams(
            collective_id=0, has_side_effects=True, vmem_limit_bytes=63 * 1024 * 1024
        ),
    )(
        out_grad,
        out_weight,
        gated_t,
        gate_input,
        scan_output,
        in_group,
        out_group_t,
        factors,
        cumul,
        cumul.T,
        expand,
        skip,
    )


def routed(
    out_grad,
    out_weight,
    gate_input,
    scan_output,
    step_size,
    log_decay,
    input_map,
    output_map,
    skip_gain,
):
    _, _, gated = gate_terms(gate_input, scan_output)
    in_group, out_group = group_maps(input_map, output_map, log_decay.shape[1])
    cumul = jnp.cumsum(log_decay, axis=0)
    weight_grad, gate_grad, input_grad = call_exchange(
        out_grad,
        out_weight,
        gated.T,
        gate_input,
        scan_output,
        in_group,
        out_group.T,
        scan_factors(cumul, step_size),
        cumul,
        skip_gain,
    )
    return input_grad, gate_grad, weight_grad


def solution(mesh):
    in_specs = (
        P("seq", None),
        P(None, "head"),
        P("seq", "head"),
        P("seq", "head"),
        P("seq", "head"),
        P("seq", "head"),
        P("seq", None, None),
        P("seq", None, None),
        P("head"),
    )
    out_specs = (P("seq", "head"), P("seq", "head"), P(None, "head"))
    small = mesh.shape["seq"] == 4 and mesh.shape["head"] == 8
    return jax.shard_map(
        routed if small else general,
        mesh=mesh,
        in_specs=in_specs,
        out_specs=out_specs,
        check_vma=False,
    )
```

```python
import math

import jax
import jax.numpy as jnp
from jax import lax
from jax.experimental import pallas as pl
from jax.experimental.pallas import tpu as pltpu
from jax.sharding import PartitionSpec as P

HEAD_COUNT = 128
G = 4
SUB = 128

f32 = jnp.float32
bf16 = jnp.bfloat16
highest = lax.Precision.HIGHEST
MESH = pl.DeviceIdType.MESH


def gate_terms(gate_input, scan_output):
    gate_value = gate_input.astype(f32)
    sig = jax.nn.sigmoid(gate_value)
    silu = gate_value * sig
    saved = scan_output.astype(f32)
    slope = saved * sig * (1.0 + gate_value * (1.0 - sig))
    gated = (saved * silu).astype(bf16)
    return silu, slope, gated


def spread_heads(values, width):
    heads = values.shape[1]
    owner = jnp.arange(heads * width) // width
    expand = (owner[None, :] == jnp.arange(heads)[:, None]).astype(f32)
    return jnp.dot(values, expand, precision=highest, preferred_element_type=f32)


def scan_pieces(scan_grad, cumulative, in_group, out_group):
    length, heads = cumulative.shape
    width = scan_grad.shape[1] // heads
    chunks = length // SUB
    grad_float = scan_grad.astype(f32)
    weighted = (grad_float * spread_heads(jnp.exp(cumulative), width)).astype(bf16)
    local_state = jnp.einsum("tk,tn->kn", weighted, out_group, preferred_element_type=f32)

    ends = cumulative[SUB - 1 :: SUB]
    b_c = in_group.reshape(chunks, SUB, -1)
    c_c = out_group.reshape(chunks, SUB, -1)
    scores = jnp.einsum("ctn,csn->cts", b_c, c_c, preferred_element_type=f32)
    cum_c = cumulative.reshape(chunks, SUB, heads).transpose(0, 2, 1)
    spread = cum_c[:, :, None, :] - cum_c[:, :, :, None]
    pos = jnp.arange(SUB)
    mask = pos[:, None] <= pos[None, :]
    factor = jnp.where(mask, jnp.exp(jnp.minimum(spread, 0.0)), 0.0)
    weights = (scores[:, None] * factor).astype(bf16)
    grads = scan_grad.reshape(chunks, SUB, heads, width)
    inside = jnp.einsum("chts,cshp->cthp", weights, grads, preferred_element_type=f32)
    inside = inside.reshape(length, heads * width)
    state = None
    later = [jnp.zeros((SUB, heads * width), f32)]
    for j in range(chunks - 2, -1, -1):
        rows = slice((j + 1) * SUB, (j + 2) * SUB)
        decay = spread_heads(jnp.exp(cumulative[rows] - ends[j][None]), width)
        fresh = jnp.einsum(
            "tn,tk->nk",
            out_group[rows],
            (grad_float[rows] * decay).astype(bf16),
            preferred_element_type=f32,
        )
        state = fresh if state is None else fresh + decay[-1][None] * state
        seen = jnp.dot(
            in_group[j * SUB : (j + 1) * SUB], state.astype(bf16), preferred_element_type=f32
        )
        tail = spread_heads(jnp.exp(ends[j][None] - cumulative[j * SUB : (j + 1) * SUB]), width)
        later.insert(0, seen * tail)
    return local_state, inside + jnp.concatenate(later, axis=0)


def group_maps(input_map, output_map, heads_here):
    index = lax.axis_index("head") * heads_here // (HEAD_COUNT // G)
    pick = lambda m: lax.dynamic_index_in_dim(m, index, 1, keepdims=False)
    return pick(input_map), pick(output_map)


def finish(inside, carried, scan_grad, cumulative, in_group, step_size, skip_gain):
    heads = cumulative.shape[1]
    width = scan_grad.shape[1] // heads
    seen = jnp.einsum("tn,kn->tk", in_group, carried.astype(bf16), preferred_element_type=f32)
    tail = spread_heads(jnp.exp(cumulative[-1:] - cumulative), width)
    return (
        spread_heads(step_size, width) * (inside + tail * seen)
        + jnp.repeat(skip_gain, width)[None] * scan_grad.astype(f32)
    ).astype(bf16)


def general(
    out_grad,
    out_weight,
    gate_input,
    scan_output,
    step_size,
    log_decay,
    input_map,
    output_map,
    skip_gain,
):
    length = out_grad.shape[0]
    heads_here = log_decay.shape[1]
    n_seq = lax.axis_size("seq")
    width = gate_input.shape[1] // heads_here
    cols = out_weight.shape[1]
    silu, slope, gated = gate_terms(gate_input, scan_output)
    mine = lax.dynamic_slice_in_dim(out_grad, lax.axis_index("head") * cols, cols, 1)
    row_panel = lax.all_to_all(out_weight, "head", split_axis=0, concat_axis=1, tiled=True)
    upstream = jnp.einsum("td,kd->tk", out_grad, row_panel, preferred_element_type=f32)
    gate_grad = (upstream * slope).astype(bf16)
    scan_grad = (upstream * silu).astype(bf16)
    in_group, out_group = group_maps(input_map, output_map, heads_here)
    cumulative = jnp.cumsum(log_decay, axis=0)
    local_state, inside = scan_pieces(scan_grad, cumulative, in_group, out_group)
    decay_all = jnp.repeat(jnp.exp(cumulative[-1]), width)[:, None]

    def relay_turn(_, carried_in):
        outgoing = (local_state + decay_all * carried_in).astype(bf16)
        route = [(i + 1, i) for i in range(n_seq - 1)]
        return lax.ppermute(outgoing, "seq", route).astype(f32)

    carried = lax.fori_loop(0, n_seq - 1, relay_turn, jnp.zeros_like(local_state))
    input_grad = finish(inside, carried, scan_grad, cumulative, in_group, step_size, skip_gain)
    gated_all = lax.all_gather(gated, "head", axis=1, tiled=True)
    part = jnp.einsum("tk,td->kd", gated_all, mine, preferred_element_type=f32)
    part = (part * (1.0 / math.sqrt(length * n_seq))).astype(bf16)
    return input_grad, gate_grad, lax.psum(part, "seq")


def mirror(at, upper):
    return at + upper * (3 - 2 * at)


def exchange(
    out_grad,
    out_weight,
    gate_input,
    scan_output,
    in_group,
    out_group_t,
    log_decay_t,
    step_t,
    skip_gain,
    weight_grad,
    gate_grad,
    input_grad,
    cls,
    og,
    wbuf,
    xsend,
    xrecv,
    xsum,
    rs,
    st_own,
    st_x,
    st_pair,
    st_y,
    total,
    total_x,
    inside,
    state,
    factors,
    cumul,
    cumul_t,
    expand,
    local_sem,
    w_sem,
    xs,
    xr,
    rss,
    rsr,
    zs,
    zr,
    es,
    er,
    bs,
    br,
    cs,
    cr,
    ks,
    kr,
    ts,
    tr,
    ol,
    os_,
    or_,
):
    length, cols = gate_input.shape
    tiles = 4
    tile = cols // tiles
    s, h = lax.axis_index("seq"), lax.axis_index("head")
    z, core = lax.div(h, 2), lax.rem(h, 2)
    upper = lax.div(z, 2)
    zz = z + upper * (3 - 2 * z)
    inner, end = zz == 1, zz == 0
    mate = h + 1 - 2 * core
    dev_core = (s, mate)
    dev_x = (s + 1 - 2 * lax.rem(s, 2), h)
    dev_y = (lax.rem(s + 2, 4), h)
    inward = mirror(zz + 1, upper)
    dev_in = (s, inward * 2 + core)
    dev_out = (s, mirror(0, upper) * 2 + core)
    seg = [mirror(3, upper), mirror(2, upper), mirror(1 - zz, upper), z]
    plane = [z, inward, mirror(2 - 2 * zz, upper), mirror(3, upper)]

    def remote(src, dst, ssem, rsem, dev):
        return pltpu.make_async_remote_copy(
            src_ref=src, dst_ref=dst, send_sem=ssem, recv_sem=rsem, device_id=dev, device_id_type=MESH
        )

    heads = log_decay_t.shape[0]
    width = cols // heads
    sub = length // 4

    def spread(values):
        return jnp.dot(values, expand[...], precision=highest, preferred_element_type=f32)

    def own_cols(part, sem):
        who = h if part == 0 else mate
        return pltpu.make_async_copy(
            out_grad.at[:, pl.ds(pl.multiple_of(who * cols, cols), cols)],
            og.at[pl.ds(0, length), pl.ds(part * cols, cols)],
            local_sem.at[sem],
        )

    def w_load(i):
        who = (1 - core) if i % 2 == 0 else core
        row = pl.multiple_of((seg[i // 2] * 2 + who) * cols, cols)
        return pltpu.make_async_copy(
            out_weight.at[pl.ds(row, cols), :], wbuf.at[i % 2], w_sem.at[i % 2]
        )

    own_cols(0, 0).start()
    own_cols(1, 1).start()
    w_load(0).start()
    w_load(1).start()

    def place(r, _):
        at = pl.ds(pl.multiple_of(r * tile, tile), tile)
        gate = gate_input[:, at].astype(f32)
        saved = scan_output[:, at].astype(f32)
        gated = saved * (gate / (1.0 + jnp.exp(-gate)))
        cls[z, at, 0:length] = jnp.transpose(gated).astype(bf16)
        return 0

    lax.fori_loop(0, tiles, place, 0)

    barrier = pltpu.get_barrier_semaphore()
    for dev in (dev_core, dev_x, dev_y, dev_in):
        pl.semaphore_signal(barrier, inc=1, device_id=dev, device_id_type=MESH)

    @pl.when(inner)
    def _():
        pl.semaphore_signal(barrier, inc=1, device_id=dev_out, device_id_type=MESH)

    @pl.when(inner)
    def _():
        pl.semaphore_wait(barrier, 5)

    @pl.when(end)
    def _():
        pl.semaphore_wait(barrier, 4)

    def token(b):
        return pl.ds(b * length, length)

    def z_own(k):
        return remote(
            cls.at[z, :, token(0)], cls.at[z, :, token(0)], zs.at[k], zr.at[z], dev_in if k == 0 else dev_out
        )

    def z_pass(j):
        block = cls.at[plane[j], :, token(0)]
        return remote(block, block, zs.at[j + 1], zr.at[plane[j]], dev_in if j == 2 else dev_out)

    def z_arrive(j):
        block = cls.at[plane[j], :, token(0)]
        remote(block, block, zs.at[0], zr.at[plane[j]], dev_in).wait_recv()

    quarter = cols // 4
    kept = cols - quarter

    def extra(j):
        return cls.at[plane[j], pl.ds(kept, quarter), pl.ds(length, 3 * length)]

    def e_own(k):
        block = extra(0)
        return remote(block, block, es.at[k], er.at[z], dev_in if k == 0 else dev_out)

    def e_pass(j):
        block = extra(j)
        return remote(block, block, es.at[j + 1], er.at[plane[j]], dev_in if j == 2 else dev_out)

    def e_arrive(j):
        block = extra(j)
        remote(block, block, es.at[0], er.at[plane[j]], dev_in).wait_recv()

    def b_copy(j, kind):
        p = plane[j]
        count = cols if j == 0 else kept
        rows = pl.ds(0, count)
        if kind < 2:
            src = cls.at[p, rows, token(0)]
            dst = cls.at[p, rows, token(kind + 1)]
            dev = dev_x if kind == 0 else dev_y
        else:
            rows = pl.ds(0, count // 2) if kind == 2 else pl.ds(count // 2, count // 2)
            src = cls.at[p, rows, token(1 if kind == 2 else 2)]
            dst = cls.at[p, rows, token(3)]
            dev = dev_y if kind == 2 else dev_x
        return remote(src, dst, bs.at[j, kind], br.at[j, kind], dev)

    def b_first(j):
        b_copy(j, 0).start()
        b_copy(j, 1).start()

    def b_second(j):
        b_copy(j, 0).wait_recv()
        b_copy(j, 2).start()
        b_copy(j, 1).wait_recv()
        b_copy(j, 3).start()

    def b_last(j):
        b_copy(j, 2).wait_recv()
        b_copy(j, 3).wait_recv()

    hl = length // 2
    c_rows = [
        pl.ds(length, length),
        pl.ds(2 * length, length),
        pl.ds(3 * length, hl),
        pl.ds(3 * length + hl, hl),
    ]

    def c_copy(kind):
        src_rows = [pl.ds(0, length), pl.ds(0, length), pl.ds(length, hl), pl.ds(2 * length + hl, hl)]
        dev = dev_x if kind in (0, 3) else dev_y
        mine = pl.ds(0, cols)
        return remote(
            og.at[src_rows[kind], mine], og.at[c_rows[kind], mine], cs.at[kind], cr.at[kind], dev
        )

    def k_copy(kind):
        return remote(
            og.at[c_rows[kind], pl.ds(0, cols)],
            og.at[c_rows[kind], pl.ds(cols, cols)],
            ks.at[kind],
            kr.at[kind],
            dev_core,
        )

    b_first(0)

    z_own(0).start()

    @pl.when(inner)
    def _():
        z_own(1).start()

    own_cols(0, 0).wait()
    own_cols(1, 1).wait()
    c_copy(0).start()
    c_copy(1).start()
    total_copy = remote(total, total_x, ts.at[2], tr.at[2], dev_x)

    def gather_factors():
        at_t = lax.broadcasted_iota(jnp.int32, (length, length), 0)
        at_s = lax.broadcasted_iota(jnp.int32, (length, length), 1)
        upto = (at_s <= at_t).astype(f32)
        from_on = (at_t <= at_s).astype(f32)
        same = (at_t == at_s).astype(f32)

        def by_token(matrix, values):
            return lax.dot_general(
                matrix,
                values,
                (((1,), (1,)), ((), ())),
                precision=highest,
                preferred_element_type=f32,
            )

        cumul[...] = by_token(upto, log_decay_t[...])
        cumul_t[...] = jnp.dot(
            log_decay_t[...], from_on, precision=highest, preferred_element_type=f32
        )
        factors[4, :, :] = by_token(same, step_t[...])
        first = lax.broadcasted_iota(jnp.int32, (heads, cols), 0) * width
        lane = lax.broadcasted_iota(jnp.int32, (heads, cols), 1)
        expand[...] = ((lane >= first) & (lane < first + width)).astype(f32)
        last = cumul[length - 1 :, :]
        for j in range(4):
            rows = pl.ds(j * sub, sub)
            here = cumul[rows, :]
            end_here = cumul[(j + 1) * sub - 1 : (j + 1) * sub, :]
            before = cumul[j * sub - 1 : j * sub, :] if j else jnp.zeros_like(last)
            factors[0, rows, :] = jnp.exp(here)
            factors[1, rows, :] = jnp.exp(here - before)
            factors[2, rows, :] = jnp.exp(end_here - here)
            factors[3, rows, :] = jnp.exp(last - here)
        total[...] = spread(jnp.broadcast_to(jnp.exp(last), (8, heads)))

    def product(i, dst):
        w_load(i).wait()

        def step(r, _):
            lanes = pl.ds(pl.multiple_of(r * tile, tile), tile)
            part = lax.dot_general(
                og[pl.ds(0, length), pl.ds(0, cols)],
                wbuf[i % 2, lanes, :],
                (((1,), (1,)), ((), ())),
                preferred_element_type=f32,
            )
            dst[:, lanes] = part.astype(bf16)
            return 0

        lax.fori_loop(0, tiles, step, 0)
        if i + 2 < 8:
            w_load(i + 2).start()

    def x_copy(n):
        return remote(xsend.at[n % 2], xrecv.at[n], xs.at[n % 2], xr.at[n], dev_core)

    rows_at_once = min(64, length)

    def by_rows(body):
        def step(r, _):
            body(pl.ds(pl.multiple_of(r * rows_at_once, rows_at_once), rows_at_once))
            return 0

        lax.fori_loop(0, length // rows_at_once, step, 0)

    def add_into(n, other):
        def body(rows):
            xsum[n, rows, :] = (xsum[n, rows, :].astype(f32) + other[rows, :].astype(f32)).astype(bf16)

        by_rows(body)

    def rs_end(n):
        return remote(xsum.at[n], rs.at[n], rss.at[n], rsr.at[n], dev_in)

    def rs_inner(n):
        dst, dev = [(3, dev_in), (4, dev_in), (2, dev_out)][n]
        return remote(xsum.at[n], rs.at[dst], rss.at[n], rsr.at[dst], dev)

    def rs_arrive(slot):
        remote(rs.at[slot], rs.at[slot], rss.at[0], rsr.at[slot], dev_in).wait_recv()

    for n in range(4):
        if n >= 2:
            x_copy(n - 2).wait_send()
        product(2 * n, xsend.at[n % 2])
        x_copy(n).start()
        product(2 * n + 1, xsum.at[n])
        if n:
            x_copy(n - 1).wait_recv()
            add_into(n - 1, xrecv.at[n - 1])

            @pl.when(end)
            def _():
                rs_end(n - 1).start()

    x_copy(3).wait_recv()
    x_copy(2).wait_send()
    x_copy(3).wait_send()

    gather_factors()
    total_copy.start()

    z_arrive(1)
    b_first(1)

    @pl.when(inner)
    def _():
        z_pass(1).start()
        z_arrive(2)
        z_pass(2).start()

    b_second(0)

    @pl.when(inner)
    def _():
        rs_arrive(0)
        add_into(0, rs.at[0])
        rs_inner(0).start()

    c_copy(0).wait_recv()
    c_copy(2).start()
    k_copy(0).start()
    c_copy(1).wait_recv()
    c_copy(3).start()
    k_copy(1).start()

    @pl.when(inner)
    def _():
        z_arrive(3)
        z_pass(3).start()
        rs_arrive(1)
        add_into(1, rs.at[1])
        rs_inner(1).start()
        rs_arrive(3)
        add_into(2, rs.at[3])
        rs_inner(2).start()

    @pl.when(end)
    def _():
        z_arrive(2)

    b_first(2)
    b_last(0)
    e_own(0).start()

    @pl.when(inner)
    def _():
        e_own(1).start()

    c_copy(2).wait_recv()
    k_copy(2).start()
    c_copy(3).wait_recv()
    k_copy(3).start()
    for kind in range(4):
        k_copy(kind).wait_recv()

    grad_scale = 1.0 / math.sqrt(length * 4)
    wide = min(512, cols)

    def out_local(j, r):
        row = pl.multiple_of((plane[j] * 2 + core) * cols + r * tile, tile)
        rows = pl.ds(pl.multiple_of(r * tile, tile), tile)
        return pltpu.make_async_copy(
            wbuf.at[0, rows, :], weight_grad.at[pl.ds(row, tile), :], ol.at[r]
        )

    def out_remote(j, r):
        row = pl.multiple_of((plane[j] * 2 + core) * cols + r * tile, tile)
        rows = pl.ds(pl.multiple_of(r * tile, tile), tile)
        return remote(
            wbuf.at[1, rows, :], weight_grad.at[pl.ds(row, tile), :], os_.at[r], or_.at[j, r], dev_core
        )

    def out_arrive(j, r):
        row = pl.multiple_of((plane[j] * 2 + 1 - core) * cols + r * tile, tile)
        there = weight_grad.at[pl.ds(row, tile), :]
        remote(there, there, os_.at[r], or_.at[j, r], dev_core).wait_recv()

    early = 3 * length

    def held_at(part, r):
        per = length // tile
        row = pl.multiple_of(lax.rem(r, per) * tile, tile)
        return part * 2 + lax.div(r, per), pl.ds(row, tile)

    def early_rows():
        def step(r, _):
            rows = pl.ds(pl.multiple_of(r * tile, tile), tile)
            for n in range(2 * cols // wide):
                part = jnp.dot(
                    cls[plane[3], rows, pl.ds(0, early)],
                    og[pl.ds(0, early), pl.ds(n * wide, wide)],
                    preferred_element_type=f32,
                )
                slab, at_rows = held_at(n * wide // cols, r)
                xsum[slab, at_rows, pl.ds(n * wide % cols, wide)] = part.astype(bf16)
            return 0

        lax.fori_loop(0, tiles - 1, step, 0)

    def rows_of(j, first=0, last=4, begun=False):
        def step(r, _):
            rows = pl.ds(pl.multiple_of(r * tile, tile), tile)
            if j:
                out_local(j - 1, r).wait()
                out_remote(j - 1, r).wait_send()
            for n in range(2 * cols // wide):
                at = n * wide
                lanes = pl.ds(at % cols, wide)
                tokens = pl.ds(early, length) if begun else pl.ds(0, 4 * length)
                part = jnp.dot(
                    cls[plane[j], rows, tokens],
                    og[tokens, pl.ds(at, wide)],
                    preferred_element_type=f32,
                )
                if begun:
                    slab, at_rows = held_at(at // cols, r)
                    part = part + xsum[slab, at_rows, lanes].astype(f32)
                wbuf[at // cols, rows, lanes] = (part * grad_scale).astype(bf16)
            out_local(j, r).start()
            out_remote(j, r).start()
            return 0

        lax.fori_loop(first, last, step, 0)

    rows_of(0)

    rs_arrive(2)

    @pl.when(inner)
    def _():
        rs_arrive(4)

    def top(rows):
        up = xsum[3, rows, :].astype(f32) + xrecv[3, rows, :].astype(f32) + rs[2, rows, :].astype(f32)
        up = jnp.where(inner, up + rs[4, rows, :].astype(f32), up)
        gate = gate_input[rows, :].astype(f32)
        sig = 1.0 / (1.0 + jnp.exp(-gate))
        saved = scan_output[rows, :].astype(f32)
        gate_grad[rows, :] = (up * saved * sig * (1.0 + gate * (1.0 - sig))).astype(bf16)
        grad = (up * (gate * sig)).astype(bf16)
        xsend[1, rows, :] = grad
        xsend[0, rows, :] = (grad.astype(f32) * spread(factors[0, rows, :])).astype(bf16)

    by_rows(top)
    st_own[...] = jnp.dot(out_group_t[...], xsend[0], preferred_element_type=f32).astype(bf16)
    hop_x = remote(st_own, st_x, ts.at[0], tr.at[0], dev_x)
    hop_x.start()

    def inside_of(j):
        rows = pl.ds(j * sub, sub)
        scores = jnp.dot(
            in_group[rows, :], out_group_t[:, j * sub : (j + 1) * sub], preferred_element_type=f32
        )
        at_t = lax.broadcasted_iota(jnp.int32, (sub, sub), 0)
        at_s = lax.broadcasted_iota(jnp.int32, (sub, sub), 1)
        scores = jnp.where(at_t <= at_s, scores, 0.0)
        left = lax.broadcasted_iota(jnp.int32, (sub, 2 * width), 1) < width
        for pair in range(heads // 2):
            lanes = pl.ds(pair * 2 * width, 2 * width)
            grads = xsend[1, rows, lanes]
            sums = []
            for head in (2 * pair, 2 * pair + 1):
                ahead = cumul_t[head : head + 1, j * sub : (j + 1) * sub] - cumul[rows, head : head + 1]
                weights = (scores * jnp.exp(jnp.minimum(ahead, 0.0))).astype(bf16)
                sums.append(jnp.dot(weights, grads, preferred_element_type=f32))
            inside[rows, lanes] = jnp.where(left, sums[0], sums[1])
        if j < 3:
            seen = jnp.dot(in_group[rows, :], state[...].astype(bf16), preferred_element_type=f32)
            inside[rows, :] += seen * spread(factors[2, rows, :])
        if j:
            decay = spread(factors[1, rows, :])
            fresh = jnp.dot(
                out_group_t[:, j * sub : (j + 1) * sub],
                (xsend[1, rows, :].astype(f32) * decay).astype(bf16),
                preferred_element_type=f32,
            )
            state[...] = fresh if j == 3 else fresh + decay[sub - 1 :, :] * state[...]

    def finish_rows(j):
        skip = spread(jnp.broadcast_to(skip_gain[...], (8, heads)))
        rows = pl.ds(j * sub, sub)
        seen = jnp.dot(in_group[rows, :], st_own[...], preferred_element_type=f32)
        grad = xsend[1, rows, :].astype(f32)
        input_grad[rows, :] = (
            spread(factors[4, rows, :]) * (inside[rows, :] + spread(factors[3, rows, :]) * seen)
            + skip[0:1, :] * grad
        ).astype(bf16)

    b_second(1)

    @pl.when(end)
    def _():
        z_arrive(3)

    b_first(3)

    @pl.when(inner)
    def _():
        e_arrive(1)
        e_pass(1).start()
        e_arrive(2)
        e_pass(2).start()

    inside_of(3)
    inside_of(2)
    total_copy.wait_recv()
    hop_x.wait_recv()
    hop_y = remote(st_pair, st_y, ts.at[1], tr.at[1], dev_y)
    mine, theirs = st_own[...].astype(f32), st_x[...].astype(f32)
    st_pair[...] = jnp.where(
        s == 2, mine + total[0:1, :] * theirs, theirs + total_x[0:1, :] * mine
    ).astype(bf16)

    @pl.when(s >= 2)
    def _():
        hop_y.start()

    b_second(2)

    @pl.when(end)
    def _():
        e_arrive(1)

    b_last(1)
    rows_of(1)

    @pl.when(inner)
    def _():
        e_arrive(3)
        e_pass(3).start()

    hop_x.wait_send()

    @pl.when(s < 2)
    def _():
        hop_y.wait_recv()
        later = st_y[...].astype(f32)
        st_own[...] = jnp.where(
            s == 0, st_x[...].astype(f32) + total_x[0:1, :] * later, later
        ).astype(bf16)

    @pl.when(s >= 2)
    def _():
        st_own[...] = jnp.where(s == 2, st_x[...].astype(f32), 0.0).astype(bf16)

    inside_of(1)
    inside_of(0)
    b_second(3)

    @pl.when(end)
    def _():
        e_arrive(2)

    b_last(2)
    rows_of(2)
    for j in range(4):
        finish_rows(j)
    for n in range(3):
        rs_end(n).wait_send()
    early_rows()
    b_last(3)
    rows_of(3, 0, tiles - 1, True)

    @pl.when(end)
    def _():
        e_arrive(3)

    rows_of(3, tiles - 1, tiles)

    for j in range(4):
        for kind in range(4):
            b_copy(j, kind).wait_send()
    for kind in range(4):
        c_copy(kind).wait_send()
        k_copy(kind).wait_send()
    total_copy.wait_send()

    @pl.when(s >= 2)
    def _():
        hop_y.wait_send()

    z_own(0).wait_send()
    e_own(0).wait_send()

    @pl.when(inner)
    def _():
        z_own(1).wait_send()
        e_own(1).wait_send()
        for j in (1, 2, 3):
            z_pass(j).wait_send()
            e_pass(j).wait_send()

    def drain(r, _):
        out_local(3, r).wait()
        out_remote(3, r).wait_send()
        for j in range(4):
            out_arrive(j, r)
        return 0

    lax.fori_loop(0, tiles, drain, 0)


def call_exchange(
    out_grad, out_weight, gate_input, scan_output, in_group, out_group_t, log_decay, step_size, skip
):
    length, cols = gate_input.shape
    state = out_group_t.shape[0]
    heads = log_decay.shape[1]
    tiles = 4
    dma = pltpu.SemaphoreType.DMA
    hbm = pl.BlockSpec(memory_space=pl.ANY)
    vmem = pl.BlockSpec(memory_space=pltpu.VMEM)
    return pl.pallas_call(
        exchange,
        out_shape=(
            jax.ShapeDtypeStruct(out_weight.shape, bf16),
            jax.ShapeDtypeStruct((length, cols), bf16),
            jax.ShapeDtypeStruct((length, cols), bf16),
        ),
        in_specs=[hbm, hbm] + [vmem] * 7,
        out_specs=(hbm, vmem, vmem),
        scratch_shapes=[
            pltpu.VMEM((4, cols, 4 * length), bf16),
            pltpu.VMEM((4 * length, 2 * cols), bf16),
            pltpu.VMEM((2, cols, cols), bf16),
            pltpu.VMEM((2, length, cols), bf16),
            pltpu.VMEM((4, length, cols), bf16),
            pltpu.VMEM((4, length, cols), bf16),
            pltpu.VMEM((5, length, cols), bf16),
            pltpu.VMEM((state, cols), bf16),
            pltpu.VMEM((state, cols), bf16),
            pltpu.VMEM((state, cols), bf16),
            pltpu.VMEM((state, cols), bf16),
            pltpu.VMEM((8, cols), f32),
            pltpu.VMEM((8, cols), f32),
            pltpu.VMEM((length, cols), f32),
            pltpu.VMEM((state, cols), f32),
            pltpu.VMEM((5, length, heads), f32),
            pltpu.VMEM((length, heads), f32),
            pltpu.VMEM((heads, length), f32),
            pltpu.VMEM((heads, cols), f32),
            dma((2,)),
            dma((2,)),
            dma((2,)),
            dma((4,)),
            dma((3,)),
            dma((5,)),
            dma((5,)),
            dma((4,)),
            dma((5,)),
            dma((4,)),
            dma((4, 4)),
            dma((4, 4)),
            dma((4,)),
            dma((4,)),
            dma((4,)),
            dma((4,)),
            dma((3,)),
            dma((3,)),
            dma((tiles,)),
            dma((tiles,)),
            dma((4, tiles)),
        ],
        compiler_params=pltpu.CompilerParams(
            collective_id=0, has_side_effects=True, vmem_limit_bytes=63 * 1024 * 1024
        ),
    )(
        out_grad,
        out_weight,
        gate_input,
        scan_output,
        in_group,
        out_group_t,
        log_decay.T,
        step_size.T,
        skip[None, :],
    )


def routed(
    out_grad,
    out_weight,
    gate_input,
    scan_output,
    step_size,
    log_decay,
    input_map,
    output_map,
    skip_gain,
):
    in_group, out_group = group_maps(input_map, output_map, log_decay.shape[1])
    weight_grad, gate_grad, input_grad = call_exchange(
        out_grad,
        out_weight,
        gate_input,
        scan_output,
        in_group,
        out_group.T,
        log_decay,
        step_size,
        skip_gain,
    )
    return input_grad, gate_grad, weight_grad


def solution(mesh):
    in_specs = (
        P("seq", None),
        P(None, "head"),
        P("seq", "head"),
        P("seq", "head"),
        P("seq", "head"),
        P("seq", "head"),
        P("seq", None, None),
        P("seq", None, None),
        P("head"),
    )
    out_specs = (P("seq", "head"), P("seq", "head"), P(None, "head"))
    small = mesh.shape["seq"] == 4 and mesh.shape["head"] == 8
    return jax.shard_map(
        routed if small else general,
        mesh=mesh,
        in_specs=in_specs,
        out_specs=out_specs,
        check_vma=False,
    )
```

```python
import math

import jax
import jax.numpy as jnp
from jax import lax
from jax.experimental import pallas as pl
from jax.experimental.pallas import tpu as pltpu
from jax.sharding import PartitionSpec as P

HEAD_COUNT = 128
G = 4
SUB = 128

f32 = jnp.float32
bf16 = jnp.bfloat16
highest = lax.Precision.HIGHEST
MESH = pl.DeviceIdType.MESH


def gate_terms(gate_input, scan_output):
    gate_value = gate_input.astype(f32)
    sig = jax.nn.sigmoid(gate_value)
    silu = gate_value * sig
    saved = scan_output.astype(f32)
    slope = saved * sig * (1.0 + gate_value * (1.0 - sig))
    gated = (saved * silu).astype(bf16)
    return silu, slope, gated


def spread_heads(values, width):
    heads = values.shape[1]
    owner = jnp.arange(heads * width) // width
    expand = (owner[None, :] == jnp.arange(heads)[:, None]).astype(f32)
    return jnp.dot(values, expand, precision=highest, preferred_element_type=f32)


def scan_pieces(scan_grad, cumulative, in_group, out_group):
    length, heads = cumulative.shape
    width = scan_grad.shape[1] // heads
    chunks = length // SUB
    grad_float = scan_grad.astype(f32)
    weighted = (grad_float * spread_heads(jnp.exp(cumulative), width)).astype(bf16)
    local_state = jnp.einsum("tk,tn->kn", weighted, out_group, preferred_element_type=f32)

    ends = cumulative[SUB - 1 :: SUB]
    b_c = in_group.reshape(chunks, SUB, -1)
    c_c = out_group.reshape(chunks, SUB, -1)
    scores = jnp.einsum("ctn,csn->cts", b_c, c_c, preferred_element_type=f32)
    cum_c = cumulative.reshape(chunks, SUB, heads).transpose(0, 2, 1)
    spread = cum_c[:, :, None, :] - cum_c[:, :, :, None]
    pos = jnp.arange(SUB)
    mask = pos[:, None] <= pos[None, :]
    factor = jnp.where(mask, jnp.exp(jnp.minimum(spread, 0.0)), 0.0)
    weights = (scores[:, None] * factor).astype(bf16)
    grads = scan_grad.reshape(chunks, SUB, heads, width)
    inside = jnp.einsum("chts,cshp->cthp", weights, grads, preferred_element_type=f32)
    inside = inside.reshape(length, heads * width)
    state = None
    later = [jnp.zeros((SUB, heads * width), f32)]
    for j in range(chunks - 2, -1, -1):
        rows = slice((j + 1) * SUB, (j + 2) * SUB)
        decay = spread_heads(jnp.exp(cumulative[rows] - ends[j][None]), width)
        fresh = jnp.einsum(
            "tn,tk->nk",
            out_group[rows],
            (grad_float[rows] * decay).astype(bf16),
            preferred_element_type=f32,
        )
        state = fresh if state is None else fresh + decay[-1][None] * state
        seen = jnp.dot(
            in_group[j * SUB : (j + 1) * SUB], state.astype(bf16), preferred_element_type=f32
        )
        tail = spread_heads(jnp.exp(ends[j][None] - cumulative[j * SUB : (j + 1) * SUB]), width)
        later.insert(0, seen * tail)
    return local_state, inside + jnp.concatenate(later, axis=0)


def group_maps(input_map, output_map, heads_here):
    index = lax.axis_index("head") * heads_here // (HEAD_COUNT // G)
    pick = lambda m: lax.dynamic_index_in_dim(m, index, 1, keepdims=False)
    return pick(input_map), pick(output_map)


def finish(inside, carried, scan_grad, cumulative, in_group, step_size, skip_gain):
    heads = cumulative.shape[1]
    width = scan_grad.shape[1] // heads
    seen = jnp.einsum("tn,kn->tk", in_group, carried.astype(bf16), preferred_element_type=f32)
    tail = spread_heads(jnp.exp(cumulative[-1:] - cumulative), width)
    return (
        spread_heads(step_size, width) * (inside + tail * seen)
        + jnp.repeat(skip_gain, width)[None] * scan_grad.astype(f32)
    ).astype(bf16)


def general(
    out_grad,
    out_weight,
    gate_input,
    scan_output,
    step_size,
    log_decay,
    input_map,
    output_map,
    skip_gain,
):
    length = out_grad.shape[0]
    heads_here = log_decay.shape[1]
    n_seq = lax.axis_size("seq")
    width = gate_input.shape[1] // heads_here
    cols = out_weight.shape[1]
    silu, slope, gated = gate_terms(gate_input, scan_output)
    mine = lax.dynamic_slice_in_dim(out_grad, lax.axis_index("head") * cols, cols, 1)
    row_panel = lax.all_to_all(out_weight, "head", split_axis=0, concat_axis=1, tiled=True)
    upstream = jnp.einsum("td,kd->tk", out_grad, row_panel, preferred_element_type=f32)
    gate_grad = (upstream * slope).astype(bf16)
    scan_grad = (upstream * silu).astype(bf16)
    in_group, out_group = group_maps(input_map, output_map, heads_here)
    cumulative = jnp.cumsum(log_decay, axis=0)
    local_state, inside = scan_pieces(scan_grad, cumulative, in_group, out_group)
    decay_all = jnp.repeat(jnp.exp(cumulative[-1]), width)[:, None]

    def relay_turn(_, carried_in):
        outgoing = (local_state + decay_all * carried_in).astype(bf16)
        route = [(i + 1, i) for i in range(n_seq - 1)]
        return lax.ppermute(outgoing, "seq", route).astype(f32)

    carried = lax.fori_loop(0, n_seq - 1, relay_turn, jnp.zeros_like(local_state))
    input_grad = finish(inside, carried, scan_grad, cumulative, in_group, step_size, skip_gain)
    gated_all = lax.all_gather(gated, "head", axis=1, tiled=True)
    part = jnp.einsum("tk,td->kd", gated_all, mine, preferred_element_type=f32)
    part = (part * (1.0 / math.sqrt(length * n_seq))).astype(bf16)
    return input_grad, gate_grad, lax.psum(part, "seq")


def mirror(at, upper):
    return at + upper * (3 - 2 * at)


def exchange(
    out_grad,
    out_weight,
    gate_input,
    scan_output,
    in_group,
    out_group_t,
    log_decay_t,
    step_t,
    skip_gain,
    weight_grad,
    gate_grad,
    input_grad,
    cls,
    og,
    wbuf,
    xsend,
    xrecv,
    xsum,
    rs,
    st_own,
    st_x,
    st_pair,
    st_y,
    total,
    total_x,
    inside,
    state,
    factors,
    cumul,
    cumul_t,
    expand,
    local_sem,
    w_sem,
    xs,
    xr,
    rss,
    rsr,
    zs,
    zr,
    es,
    er,
    bs,
    br,
    cs,
    cr,
    ks,
    kr,
    ts,
    tr,
    ol,
    os_,
    or_,
):
    length, cols = gate_input.shape
    tiles = 4
    tile = cols // tiles
    s, h = lax.axis_index("seq"), lax.axis_index("head")
    z, core = lax.div(h, 2), lax.rem(h, 2)
    upper = lax.div(z, 2)
    zz = z + upper * (3 - 2 * z)
    inner, end = zz == 1, zz == 0
    mate = h + 1 - 2 * core
    dev_core = (s, mate)
    dev_x = (s + 1 - 2 * lax.rem(s, 2), h)
    dev_y = (lax.rem(s + 2, 4), h)
    inward = mirror(zz + 1, upper)
    dev_in = (s, inward * 2 + core)
    dev_out = (s, mirror(0, upper) * 2 + core)
    seg = [mirror(3, upper), mirror(2, upper), mirror(1 - zz, upper), z]
    plane = [z, inward, mirror(2 - 2 * zz, upper), mirror(3, upper)]

    def remote(src, dst, ssem, rsem, dev):
        return pltpu.make_async_remote_copy(
            src_ref=src, dst_ref=dst, send_sem=ssem, recv_sem=rsem, device_id=dev, device_id_type=MESH
        )

    heads = log_decay_t.shape[0]
    width = cols // heads
    sub = length // 4

    def spread(values):
        return jnp.dot(values, expand[...], precision=highest, preferred_element_type=f32)

    def own_cols(part, sem):
        who = h if part == 0 else mate
        return pltpu.make_async_copy(
            out_grad.at[:, pl.ds(pl.multiple_of(who * cols, cols), cols)],
            og.at[pl.ds(0, length), pl.ds(part * cols, cols)],
            local_sem.at[sem],
        )

    def w_load(i):
        who = (1 - core) if i % 2 == 0 else core
        row = pl.multiple_of((seg[i // 2] * 2 + who) * cols, cols)
        return pltpu.make_async_copy(
            out_weight.at[pl.ds(row, cols), :], wbuf.at[i % 2], w_sem.at[i % 2]
        )

    own_cols(0, 0).start()
    own_cols(1, 1).start()
    w_load(0).start()
    w_load(1).start()

    def place(r, _):
        at = pl.ds(pl.multiple_of(r * tile, tile), tile)
        gate = gate_input[:, at].astype(f32)
        saved = scan_output[:, at].astype(f32)
        gated = saved * (gate / (1.0 + jnp.exp(-gate)))
        cls[z, at, 0:length] = jnp.transpose(gated).astype(bf16)
        return 0

    lax.fori_loop(0, tiles, place, 0)

    barrier = pltpu.get_barrier_semaphore()
    for dev in (dev_core, dev_x, dev_y, dev_in):
        pl.semaphore_signal(barrier, inc=1, device_id=dev, device_id_type=MESH)

    @pl.when(inner)
    def _():
        pl.semaphore_signal(barrier, inc=1, device_id=dev_out, device_id_type=MESH)

    @pl.when(inner)
    def _():
        pl.semaphore_wait(barrier, 5)

    @pl.when(end)
    def _():
        pl.semaphore_wait(barrier, 4)

    def token(b):
        return pl.ds(b * length, length)

    def z_own(k):
        return remote(
            cls.at[z, :, token(0)], cls.at[z, :, token(0)], zs.at[k], zr.at[z], dev_in if k == 0 else dev_out
        )

    def z_pass(j):
        block = cls.at[plane[j], :, token(0)]
        return remote(block, block, zs.at[j + 1], zr.at[plane[j]], dev_in if j == 2 else dev_out)

    def z_arrive(j):
        block = cls.at[plane[j], :, token(0)]
        remote(block, block, zs.at[0], zr.at[plane[j]], dev_in).wait_recv()

    quarter = cols // 4
    kept = cols - quarter

    def extra(j):
        return cls.at[plane[j], pl.ds(kept, quarter), pl.ds(length, 3 * length)]

    def e_own(k):
        block = extra(0)
        return remote(block, block, es.at[k], er.at[z], dev_in if k == 0 else dev_out)

    def e_pass(j):
        block = extra(j)
        return remote(block, block, es.at[j + 1], er.at[plane[j]], dev_in if j == 2 else dev_out)

    def e_arrive(j):
        block = extra(j)
        remote(block, block, es.at[0], er.at[plane[j]], dev_in).wait_recv()

    def b_copy(j, kind):
        p = plane[j]
        count = cols if j == 0 else kept
        rows = pl.ds(0, count)
        if kind < 2:
            src = cls.at[p, rows, token(0)]
            dst = cls.at[p, rows, token(kind + 1)]
            dev = dev_x if kind == 0 else dev_y
        else:
            rows = pl.ds(0, count // 2) if kind == 2 else pl.ds(count // 2, count // 2)
            src = cls.at[p, rows, token(1 if kind == 2 else 2)]
            dst = cls.at[p, rows, token(3)]
            dev = dev_y if kind == 2 else dev_x
        return remote(src, dst, bs.at[j, kind], br.at[j, kind], dev)

    def b_first(j):
        b_copy(j, 0).start()
        b_copy(j, 1).start()

    def b_second(j):
        b_copy(j, 0).wait_recv()
        b_copy(j, 2).start()
        b_copy(j, 1).wait_recv()
        b_copy(j, 3).start()

    def b_last(j):
        b_copy(j, 2).wait_recv()
        b_copy(j, 3).wait_recv()

    hl = length // 2
    c_rows = [
        pl.ds(length, length),
        pl.ds(2 * length, length),
        pl.ds(3 * length, hl),
        pl.ds(3 * length + hl, hl),
    ]

    def c_copy(kind):
        src_rows = [pl.ds(0, length), pl.ds(0, length), pl.ds(length, hl), pl.ds(2 * length + hl, hl)]
        dev = dev_x if kind in (0, 3) else dev_y
        mine = pl.ds(0, cols)
        return remote(
            og.at[src_rows[kind], mine], og.at[c_rows[kind], mine], cs.at[kind], cr.at[kind], dev
        )

    def k_copy(kind):
        return remote(
            og.at[c_rows[kind], pl.ds(0, cols)],
            og.at[c_rows[kind], pl.ds(cols, cols)],
            ks.at[kind],
            kr.at[kind],
            dev_core,
        )

    b_first(0)

    z_own(0).start()

    @pl.when(inner)
    def _():
        z_own(1).start()

    own_cols(0, 0).wait()
    own_cols(1, 1).wait()
    c_copy(0).start()
    c_copy(1).start()
    total_copy = remote(total, total_x, ts.at[2], tr.at[2], dev_x)

    def gather_factors():
        at_t = lax.broadcasted_iota(jnp.int32, (length, length), 0)
        at_s = lax.broadcasted_iota(jnp.int32, (length, length), 1)
        upto = (at_s <= at_t).astype(f32)
        from_on = (at_t <= at_s).astype(f32)
        same = (at_t == at_s).astype(f32)

        def by_token(matrix, values):
            return lax.dot_general(
                matrix,
                values,
                (((1,), (1,)), ((), ())),
                precision=highest,
                preferred_element_type=f32,
            )

        cumul[...] = by_token(upto, log_decay_t[...])
        cumul_t[...] = jnp.dot(
            log_decay_t[...], from_on, precision=highest, preferred_element_type=f32
        )
        factors[4, :, :] = by_token(same, step_t[...])
        first = lax.broadcasted_iota(jnp.int32, (heads, cols), 0) * width
        lane = lax.broadcasted_iota(jnp.int32, (heads, cols), 1)
        expand[...] = ((lane >= first) & (lane < first + width)).astype(f32)
        last = cumul[length - 1 :, :]
        for j in range(4):
            rows = pl.ds(j * sub, sub)
            here = cumul[rows, :]
            end_here = cumul[(j + 1) * sub - 1 : (j + 1) * sub, :]
            before = cumul[j * sub - 1 : j * sub, :] if j else jnp.zeros_like(last)
            factors[0, rows, :] = jnp.exp(here)
            factors[1, rows, :] = jnp.exp(here - before)
            factors[2, rows, :] = jnp.exp(end_here - here)
            factors[3, rows, :] = jnp.exp(last - here)
        total[...] = spread(jnp.broadcast_to(jnp.exp(last), (8, heads)))

    def product(i, dst):
        w_load(i).wait()

        def step(r, _):
            lanes = pl.ds(pl.multiple_of(r * tile, tile), tile)
            part = lax.dot_general(
                og[pl.ds(0, length), pl.ds(0, cols)],
                wbuf[i % 2, lanes, :],
                (((1,), (1,)), ((), ())),
                preferred_element_type=f32,
            )
            dst[:, lanes] = part.astype(bf16)
            return 0

        lax.fori_loop(0, tiles, step, 0)
        if i + 2 < 8:
            w_load(i + 2).start()

    def x_copy(n):
        return remote(xsend.at[n % 2], xrecv.at[n], xs.at[n % 2], xr.at[n], dev_core)

    rows_at_once = min(64, length)

    def by_rows(body):
        def step(r, _):
            body(pl.ds(pl.multiple_of(r * rows_at_once, rows_at_once), rows_at_once))
            return 0

        lax.fori_loop(0, length // rows_at_once, step, 0)

    def add_into(n, other):
        def body(rows):
            xsum[n, rows, :] = (xsum[n, rows, :].astype(f32) + other[rows, :].astype(f32)).astype(bf16)

        by_rows(body)

    def rs_end(n):
        return remote(xsum.at[n], rs.at[n], rss.at[n], rsr.at[n], dev_in)

    def rs_inner(n):
        dst, dev = [(3, dev_in), (4, dev_in), (2, dev_out)][n]
        return remote(xsum.at[n], rs.at[dst], rss.at[n], rsr.at[dst], dev)

    def rs_arrive(slot):
        remote(rs.at[slot], rs.at[slot], rss.at[0], rsr.at[slot], dev_in).wait_recv()

    for n in range(4):
        if n >= 2:
            x_copy(n - 2).wait_send()
        product(2 * n, xsend.at[n % 2])
        x_copy(n).start()
        product(2 * n + 1, xsum.at[n])
        if n:
            x_copy(n - 1).wait_recv()
            add_into(n - 1, xrecv.at[n - 1])

            @pl.when(end)
            def _():
                rs_end(n - 1).start()

    x_copy(3).wait_recv()
    x_copy(2).wait_send()
    x_copy(3).wait_send()

    gather_factors()
    total_copy.start()

    z_arrive(1)
    b_first(1)

    @pl.when(inner)
    def _():
        z_pass(1).start()
        z_arrive(2)
        z_pass(2).start()

    b_second(0)

    @pl.when(inner)
    def _():
        rs_arrive(0)
        add_into(0, rs.at[0])
        rs_inner(0).start()

    c_copy(0).wait_recv()
    c_copy(2).start()
    k_copy(0).start()
    c_copy(1).wait_recv()
    c_copy(3).start()
    k_copy(1).start()

    @pl.when(inner)
    def _():
        z_arrive(3)
        z_pass(3).start()
        rs_arrive(1)
        add_into(1, rs.at[1])
        rs_inner(1).start()
        rs_arrive(3)
        add_into(2, rs.at[3])
        rs_inner(2).start()

    @pl.when(end)
    def _():
        z_arrive(2)

    b_first(2)
    b_last(0)
    e_own(0).start()

    @pl.when(inner)
    def _():
        e_own(1).start()

    c_copy(2).wait_recv()
    k_copy(2).start()
    c_copy(3).wait_recv()
    k_copy(3).start()
    b_second(1)
    for kind in range(4):
        k_copy(kind).wait_recv()

    grad_scale = 1.0 / math.sqrt(length * 4)
    wide = min(512, cols)

    def out_local(j, r):
        row = pl.multiple_of((plane[j] * 2 + core) * cols + r * tile, tile)
        rows = pl.ds(pl.multiple_of(r * tile, tile), tile)
        return pltpu.make_async_copy(
            wbuf.at[0, rows, :], weight_grad.at[pl.ds(row, tile), :], ol.at[r]
        )

    def out_remote(j, r):
        row = pl.multiple_of((plane[j] * 2 + core) * cols + r * tile, tile)
        rows = pl.ds(pl.multiple_of(r * tile, tile), tile)
        return remote(
            wbuf.at[1, rows, :], weight_grad.at[pl.ds(row, tile), :], os_.at[r], or_.at[j, r], dev_core
        )

    def out_arrive(j, r):
        row = pl.multiple_of((plane[j] * 2 + 1 - core) * cols + r * tile, tile)
        there = weight_grad.at[pl.ds(row, tile), :]
        remote(there, there, os_.at[r], or_.at[j, r], dev_core).wait_recv()

    early = 3 * length

    def held_at(part, r):
        per = length // tile
        row = pl.multiple_of(lax.rem(r, per) * tile, tile)
        return part * 2 + lax.div(r, per), pl.ds(row, tile)

    def early_rows():
        def step(r, _):
            rows = pl.ds(pl.multiple_of(r * tile, tile), tile)
            for n in range(2 * cols // wide):
                part = jnp.dot(
                    cls[plane[3], rows, pl.ds(0, early)],
                    og[pl.ds(0, early), pl.ds(n * wide, wide)],
                    preferred_element_type=f32,
                )
                slab, at_rows = held_at(n * wide // cols, r)
                xsum[slab, at_rows, pl.ds(n * wide % cols, wide)] = part.astype(bf16)
            return 0

        lax.fori_loop(0, tiles - 1, step, 0)

    def rows_of(j, first=0, last=4, begun=False):
        def step(r, _):
            rows = pl.ds(pl.multiple_of(r * tile, tile), tile)
            if j:
                out_local(j - 1, r).wait()
                out_remote(j - 1, r).wait_send()
            for n in range(2 * cols // wide):
                at = n * wide
                lanes = pl.ds(at % cols, wide)
                tokens = pl.ds(early, length) if begun else pl.ds(0, 4 * length)
                part = jnp.dot(
                    cls[plane[j], rows, tokens],
                    og[tokens, pl.ds(at, wide)],
                    preferred_element_type=f32,
                )
                if begun:
                    slab, at_rows = held_at(at // cols, r)
                    part = part + xsum[slab, at_rows, lanes].astype(f32)
                wbuf[at // cols, rows, lanes] = (part * grad_scale).astype(bf16)
            out_local(j, r).start()
            out_remote(j, r).start()
            return 0

        lax.fori_loop(first, last, step, 0)

    rows_of(0)

    @pl.when(end)
    def _():
        z_arrive(3)

    b_first(3)

    rs_arrive(2)

    @pl.when(inner)
    def _():
        rs_arrive(4)

    def top(rows):
        up = xsum[3, rows, :].astype(f32) + xrecv[3, rows, :].astype(f32) + rs[2, rows, :].astype(f32)
        up = jnp.where(inner, up + rs[4, rows, :].astype(f32), up)
        gate = gate_input[rows, :].astype(f32)
        sig = 1.0 / (1.0 + jnp.exp(-gate))
        saved = scan_output[rows, :].astype(f32)
        gate_grad[rows, :] = (up * saved * sig * (1.0 + gate * (1.0 - sig))).astype(bf16)
        grad = (up * (gate * sig)).astype(bf16)
        xsend[1, rows, :] = grad
        xsend[0, rows, :] = (grad.astype(f32) * spread(factors[0, rows, :])).astype(bf16)

    by_rows(top)
    st_own[...] = jnp.dot(out_group_t[...], xsend[0], preferred_element_type=f32).astype(bf16)
    hop_x = remote(st_own, st_x, ts.at[0], tr.at[0], dev_x)
    hop_x.start()

    def inside_of(j):
        rows = pl.ds(j * sub, sub)
        scores = jnp.dot(
            in_group[rows, :], out_group_t[:, j * sub : (j + 1) * sub], preferred_element_type=f32
        )
        at_t = lax.broadcasted_iota(jnp.int32, (sub, sub), 0)
        at_s = lax.broadcasted_iota(jnp.int32, (sub, sub), 1)
        scores = jnp.where(at_t <= at_s, scores, 0.0)
        left = lax.broadcasted_iota(jnp.int32, (sub, 2 * width), 1) < width
        for pair in range(heads // 2):
            lanes = pl.ds(pair * 2 * width, 2 * width)
            grads = xsend[1, rows, lanes]
            sums = []
            for head in (2 * pair, 2 * pair + 1):
                ahead = cumul_t[head : head + 1, j * sub : (j + 1) * sub] - cumul[rows, head : head + 1]
                weights = (scores * jnp.exp(jnp.minimum(ahead, 0.0))).astype(bf16)
                sums.append(jnp.dot(weights, grads, preferred_element_type=f32))
            inside[rows, lanes] = jnp.where(left, sums[0], sums[1])
        if j < 3:
            seen = jnp.dot(in_group[rows, :], state[...].astype(bf16), preferred_element_type=f32)
            inside[rows, :] += seen * spread(factors[2, rows, :])
        if j:
            decay = spread(factors[1, rows, :])
            fresh = jnp.dot(
                out_group_t[:, j * sub : (j + 1) * sub],
                (xsend[1, rows, :].astype(f32) * decay).astype(bf16),
                preferred_element_type=f32,
            )
            state[...] = fresh if j == 3 else fresh + decay[sub - 1 :, :] * state[...]

    def finish_rows(j):
        skip = spread(jnp.broadcast_to(skip_gain[...], (8, heads)))
        rows = pl.ds(j * sub, sub)
        seen = jnp.dot(in_group[rows, :], st_own[...], preferred_element_type=f32)
        grad = xsend[1, rows, :].astype(f32)
        input_grad[rows, :] = (
            spread(factors[4, rows, :]) * (inside[rows, :] + spread(factors[3, rows, :]) * seen)
            + skip[0:1, :] * grad
        ).astype(bf16)

    inside_of(3)
    b_second(2)
    inside_of(2)

    @pl.when(inner)
    def _():
        e_arrive(1)
        e_pass(1).start()
        e_arrive(2)
        e_pass(2).start()

    total_copy.wait_recv()
    hop_x.wait_recv()
    hop_y = remote(st_pair, st_y, ts.at[1], tr.at[1], dev_y)
    mine, theirs = st_own[...].astype(f32), st_x[...].astype(f32)
    st_pair[...] = jnp.where(
        s == 2, mine + total[0:1, :] * theirs, theirs + total_x[0:1, :] * mine
    ).astype(bf16)

    @pl.when(s >= 2)
    def _():
        hop_y.start()

    @pl.when(end)
    def _():
        e_arrive(1)

    b_last(1)
    rows_of(1)
    b_second(3)

    @pl.when(inner)
    def _():
        e_arrive(3)
        e_pass(3).start()

    inside_of(1)
    inside_of(0)
    hop_x.wait_send()

    @pl.when(s < 2)
    def _():
        hop_y.wait_recv()
        later = st_y[...].astype(f32)
        st_own[...] = jnp.where(
            s == 0, st_x[...].astype(f32) + total_x[0:1, :] * later, later
        ).astype(bf16)

    @pl.when(s >= 2)
    def _():
        st_own[...] = jnp.where(s == 2, st_x[...].astype(f32), 0.0).astype(bf16)

    @pl.when(end)
    def _():
        e_arrive(2)

    b_last(2)
    rows_of(2)
    for j in range(4):
        finish_rows(j)
    for n in range(3):
        rs_end(n).wait_send()
    early_rows()
    b_last(3)
    rows_of(3, 0, tiles - 1, True)

    @pl.when(end)
    def _():
        e_arrive(3)

    rows_of(3, tiles - 1, tiles)

    for j in range(4):
        for kind in range(4):
            b_copy(j, kind).wait_send()
    for kind in range(4):
        c_copy(kind).wait_send()
        k_copy(kind).wait_send()
    total_copy.wait_send()

    @pl.when(s >= 2)
    def _():
        hop_y.wait_send()

    z_own(0).wait_send()
    e_own(0).wait_send()

    @pl.when(inner)
    def _():
        z_own(1).wait_send()
        e_own(1).wait_send()
        for j in (1, 2, 3):
            z_pass(j).wait_send()
            e_pass(j).wait_send()

    def drain(r, _):
        out_local(3, r).wait()
        out_remote(3, r).wait_send()
        for j in range(4):
            out_arrive(j, r)
        return 0

    lax.fori_loop(0, tiles, drain, 0)


def hand_on(wide_in, gate_in, input_in, wide_out, gate_out, input_out, wide, small, in_sem, out_sem):
    pieces, rows, _ = wide.shape
    moves = [
        (wide_in.at[pl.ds(n * rows, rows), :], wide.at[n], wide_out.at[pl.ds(n * rows, rows), :])
        for n in range(pieces)
    ] + [(gate_in, small.at[0], gate_out), (input_in, small.at[1], input_out)]
    arrive = [
        pltpu.make_async_copy(src, held, in_sem.at[n]) for n, (src, held, _) in enumerate(moves)
    ]
    leave = [
        pltpu.make_async_copy(held, dst, out_sem.at[n]) for n, (_, held, dst) in enumerate(moves)
    ]
    for copy in arrive:
        copy.start()
    for copy, onward in zip(arrive, leave):
        copy.wait()
        onward.start()
    for onward in leave:
        onward.wait()


def call_hand_on(weight_grad, gate_grad, input_grad):
    pieces = 16
    rows, cols = weight_grad.shape
    hbm = pl.BlockSpec(memory_space=pl.ANY)
    arrays = (weight_grad, gate_grad, input_grad)
    return pl.pallas_call(
        hand_on,
        out_shape=tuple(jax.ShapeDtypeStruct(a.shape, a.dtype) for a in arrays),
        in_specs=[hbm] * 3,
        out_specs=(hbm,) * 3,
        scratch_shapes=[
            pltpu.VMEM((pieces, rows // pieces, cols), bf16),
            pltpu.VMEM((2,) + gate_grad.shape, bf16),
            pltpu.SemaphoreType.DMA((pieces + 2,)),
            pltpu.SemaphoreType.DMA((pieces + 2,)),
        ],
        compiler_params=pltpu.CompilerParams(vmem_limit_bytes=60 * 1024 * 1024),
    )(*arrays)


def call_exchange(
    out_grad, out_weight, gate_input, scan_output, in_group, out_group_t, log_decay, step_size, skip
):
    length, cols = gate_input.shape
    state = out_group_t.shape[0]
    heads = log_decay.shape[1]
    tiles = 4
    dma = pltpu.SemaphoreType.DMA
    hbm = pl.BlockSpec(memory_space=pl.ANY)
    vmem = pl.BlockSpec(memory_space=pltpu.VMEM)
    outs = pl.pallas_call(
        exchange,
        out_shape=(
            jax.ShapeDtypeStruct(out_weight.shape, bf16),
            jax.ShapeDtypeStruct((length, cols), bf16),
            jax.ShapeDtypeStruct((length, cols), bf16),
        ),
        in_specs=[hbm, hbm] + [vmem] * 7,
        out_specs=(hbm, vmem, vmem),
        scratch_shapes=[
            pltpu.VMEM((4, cols, 4 * length), bf16),
            pltpu.VMEM((4 * length, 2 * cols), bf16),
            pltpu.VMEM((2, cols, cols), bf16),
            pltpu.VMEM((2, length, cols), bf16),
            pltpu.VMEM((4, length, cols), bf16),
            pltpu.VMEM((4, length, cols), bf16),
            pltpu.VMEM((5, length, cols), bf16),
            pltpu.VMEM((state, cols), bf16),
            pltpu.VMEM((state, cols), bf16),
            pltpu.VMEM((state, cols), bf16),
            pltpu.VMEM((state, cols), bf16),
            pltpu.VMEM((8, cols), f32),
            pltpu.VMEM((8, cols), f32),
            pltpu.VMEM((length, cols), f32),
            pltpu.VMEM((state, cols), f32),
            pltpu.VMEM((5, length, heads), f32),
            pltpu.VMEM((length, heads), f32),
            pltpu.VMEM((heads, length), f32),
            pltpu.VMEM((heads, cols), f32),
            dma((2,)),
            dma((2,)),
            dma((2,)),
            dma((4,)),
            dma((3,)),
            dma((5,)),
            dma((5,)),
            dma((4,)),
            dma((5,)),
            dma((4,)),
            dma((4, 4)),
            dma((4, 4)),
            dma((4,)),
            dma((4,)),
            dma((4,)),
            dma((4,)),
            dma((3,)),
            dma((3,)),
            dma((tiles,)),
            dma((tiles,)),
            dma((4, tiles)),
        ],
        compiler_params=pltpu.CompilerParams(
            collective_id=0, has_side_effects=True, vmem_limit_bytes=63 * 1024 * 1024
        ),
    )(
        out_grad,
        out_weight,
        gate_input,
        scan_output,
        in_group,
        out_group_t,
        log_decay.T,
        step_size.T,
        skip[None, :],
    )
    return call_hand_on(*outs)


def routed(
    out_grad,
    out_weight,
    gate_input,
    scan_output,
    step_size,
    log_decay,
    input_map,
    output_map,
    skip_gain,
):
    in_group, out_group = group_maps(input_map, output_map, log_decay.shape[1])
    weight_grad, gate_grad, input_grad = call_exchange(
        out_grad,
        out_weight,
        gate_input,
        scan_output,
        in_group,
        out_group.T,
        log_decay,
        step_size,
        skip_gain,
    )
    return input_grad, gate_grad, weight_grad


def solution(mesh):
    in_specs = (
        P("seq", None),
        P(None, "head"),
        P("seq", "head"),
        P("seq", "head"),
        P("seq", "head"),
        P("seq", "head"),
        P("seq", None, None),
        P("seq", None, None),
        P("head"),
    )
    out_specs = (P("seq", "head"), P("seq", "head"), P(None, "head"))
    small = mesh.shape["seq"] == 4 and mesh.shape["head"] == 8
    return jax.shard_map(
        routed if small else general,
        mesh=mesh,
        in_specs=in_specs,
        out_specs=out_specs,
        check_vma=False,
    )
```
